512 devices in a mesh: gy: 32 (over y, x, core), gz: 16 (over z).
Axes of the slice: x: 4, y: 4, z: 16, core: 2. Of those that a mesh axis runs over, the one named last changes fastest.
Arguments:
- strain: float32 [6, 192, 192, 512], P(None, 'gy', 'gz'), may hold values from -8 to 8
- phase: int32 [192, 192, 512], P('gy', 'gz'), may hold values from 0 to 15
- density: float32 [16], replicated, may hold values from 0.1 to 1
- target_stress: float32 [6], replicated, may hold values from -1.5 to 1.5
Outputs:
- next_strain: float32 [6, 192, 192, 512], P(None, 'gy', 'gz')
The draws below stay inside these ranges and needn't reach their ends.
All inputs are finite; a program needn't handle non-finite values.
Results may differ from the reference program's by a relative error of at most 0.0001.
Values sent between devices are 32-bit elements; how exact they have to be, the bound alone decides.
A program may use at most 128 MiB of HBM per device.

```python
import math
import jax
import jax.numpy as jnp

NX = 512
NY = 192
NZ = 192
LEVELS = 16


def draw_strain(key, part):
    key = jax.random.fold_in(key, 7)
    jitter_key = jax.random.fold_in(key, 0)
    full_shape = (6, NY, NZ, NX)
    rows_y = jnp.arange(NY, dtype=jnp.float32) / (NY - 1)
    rows_z = jnp.arange(NZ, dtype=jnp.float32) / (NZ - 1)
    jitter = jnp.clip(jax.random.normal(jitter_key, full_shape, jnp.float32), -4.0, 4.0)
    rise_rate = 2.0
    profile = (1.0 + rise_rate * rows_y)[:, None, None] * (1.0 + 2.0 * rows_z)[None, :, None] * 0.25
    offsets = jnp.array([0.6, -0.4, 0.3, 0.2, -0.3, 0.5], jnp.float32)
    return jitter + offsets[:, None, None, None] * profile[None]


def set_ends(result, stream_key, least, high):
    extent = result.shape
    index_at = [jax.random.randint(jax.random.fold_in(stream_key, axis), (), 0, extent[axis]) for axis in range(len(extent))]
    result = result.at[tuple(index_at)].set(least)
    longest = extent.index(max(extent))
    index_at[longest] = (index_at[longest] + 1) % extent[longest]
    return result.at[tuple(index_at)].set(high)


def bell_draw(rng, dims, width, most, kind=jnp.bfloat16):
    result = jax.random.normal(rng, dims, jnp.float32) * width
    return jnp.minimum(jnp.maximum(result, -most), most).astype(kind)


def setup_inputs(seed: int = 0) -> dict:
    key_of = jax.random.split(jax.random.key(seed), 5)
    strain = draw_strain(jax.random.fold_in(key_of[4], 71), 0)
    phase = set_ends(jax.random.randint(key_of[1], (NY, NZ, NX), 0, LEVELS), jax.random.fold_in(key_of[1], 1), 0, LEVELS - 1).astype(jnp.int32)
    density = jnp.clip(jnp.exp(jax.random.uniform(key_of[2], (LEVELS,), jnp.float32, math.log(0.1), math.log(1.0))), 0.1, 1.0)
    target_stress = bell_draw(key_of[3], (6,), 0.3, 1.5, jnp.float32)
    return {"strain": strain, "phase": phase, "density": density, "target_stress": target_stress}


LAME_SOLID = 0.5769230769
SHEAR_SOLID = 0.3846153846
PAIRS = ((0, 0), (1, 1), (2, 2), (1, 2), (0, 2), (0, 1))
INDEX_MAP = ((0, 5, 4), (5, 1, 3), (4, 3, 2))


def signed_wave(length):
    wave_ids = jnp.arange(length, dtype=jnp.int32)
    return jnp.where(wave_ids > length // 2, wave_ids - length, wave_ids)


def reference(strain, phase, density, target_stress):
    stiff_scale = density ** 3
    stiffness = stiff_scale[phase]
    lame_cell = LAME_SOLID * stiffness
    shear_cell = SHEAR_SOLID * stiffness
    middle = 0.5 * (jnp.min(stiff_scale) + jnp.max(stiff_scale))
    lame_ref = LAME_SOLID * middle
    shear_ref = SHEAR_SOLID * middle
    strain_trace = strain[0] + strain[1] + strain[2]
    diagonal = (jnp.arange(6) < 3).astype(jnp.float32)
    diagonal_grid = diagonal[:, None, None, None]
    stress = diagonal_grid * (lame_cell * strain_trace)[None] + 2.0 * shear_cell[None] * strain
    polarize = diagonal_grid * ((lame_cell - lame_ref) * strain_trace)[None] + 2.0 * (shear_cell - shear_ref)[None] * strain
    mean_strain = jnp.mean(strain, axis=(1, 2, 3))
    mean_stress = jnp.mean(stress, axis=(1, 2, 3))
    excess = target_stress - mean_stress
    excess_trace = excess[0] + excess[1] + excess[2]
    macro_strain = mean_strain + (excess - diagonal * lame_ref / (3.0 * lame_ref + 2.0 * shear_ref) * excess_trace) / (2.0 * shear_ref)
    wave_y = signed_wave(NY)[:, None, None]
    wave_z = signed_wave(NZ)[None, :, None]
    wave_x = signed_wave(NX)[None, None, :]
    frequency = (wave_x / NX, wave_y / NY, wave_z / NZ)
    keep_mask = (wave_x != NX // 2) & (wave_y != NY // 2) & (wave_z != NZ // 2)
    keep_mask = keep_mask & jnp.logical_not((wave_x == 0) & (wave_y == 0) & (wave_z == 0))
    norm_sq = frequency[0] ** 2 + frequency[1] ** 2 + frequency[2] ** 2
    safe_norm = jnp.where(keep_mask, norm_sq, 1.0)
    spectra = [jnp.fft.fftn(polarize[c]) for c in range(6)]
    vector = [sum(spectra[INDEX_MAP[i][j]] * frequency[j] for j in range(3)) for i in range(3)]
    projected = frequency[0] * vector[0] + frequency[1] * vector[1] + frequency[2] * vector[2]
    scaled = [jnp.where(keep_mask, vector[i] / (2.0 * shear_ref * safe_norm), 0.0) for i in range(3)]
    coupling = (lame_ref + shear_ref) / (shear_ref * (lame_ref + 2.0 * shear_ref))
    fourth = jnp.where(keep_mask, coupling * projected / (safe_norm * safe_norm), 0.0)
    outputs = []
    for c in range(6):
        i, j = PAIRS[c]
        green_term = frequency[i] * scaled[j] + frequency[j] * scaled[i] - frequency[i] * frequency[j] * fourth
        fluctuation = jnp.real(jnp.fft.ifftn(green_term)).astype(jnp.float32)
        outputs.append(macro_strain[c] - fluctuation)
    return jnp.stack(outputs)
```

```python
import math

import jax
import jax.numpy as jnp
import ml_dtypes
import numpy as np
from jax import lax
from jax.experimental import pallas as pl
from jax.experimental.pallas import tpu as pltpu
from jax.sharding import PartitionSpec as P

NX, NY, NZ = 512, 192, 192
GY, GZ = 32, 16
YL, ZL = NY // GY, NZ // GZ
VOXELS = float(NX * NY * NZ)
LAME_SOLID = 0.5769230769
SHEAR_SOLID = 0.3846153846
MESH = pl.DeviceIdType.MESH
F32, BF16 = jnp.float32, jnp.bfloat16
TILES = 9
FORWARD = ((0, 5), (5, 9))
BACKWARD = ((0, 4), (4, 9))


def split_table(table, axis):
    high = table.astype(np.float32).astype(ml_dtypes.bfloat16)
    low = (table - high.astype(np.float64)).astype(np.float32).astype(ml_dtypes.bfloat16)
    return np.concatenate([high, high, low], axis=axis)


def wave(rows, columns, length):
    angle = 2.0 * math.pi / length * ((np.asarray(rows)[:, None] * np.asarray(columns)[None, :]) % length)
    return np.cos(angle), np.sin(angle)


def tables():
    kx = np.array([d * 16 + h * 8 + k for h in range(2) for d in range(GZ) for _ in range(2) for k in range(8)])
    imag = np.array([r for _ in range(2) for _ in range(GZ) for r in range(2) for _ in range(8)])
    cosine, sine = wave(np.arange(NX), kx, NX)
    x_table = np.where(imag[None, :] == 0, cosine, -sine)
    x_forward = split_table(x_table, 0)
    x_back = np.stack([split_table(x_table.T[h * 256 : (h + 1) * 256], 0) for h in range(2)])

    z_rows = np.arange(GZ * 16)
    z_of, z_ok = (z_rows // 16) * ZL + np.minimum(z_rows % 16, ZL - 1), z_rows % 16 < ZL
    k_rows = np.arange(GY * 8)
    k_of, k_ok = (k_rows // 8) * 6 + np.minimum(k_rows % 8, 5), k_rows % 8 < 6
    cosine, sine = wave(k_of, z_of, NZ)
    ok = k_ok[:, None] & z_ok[None, :]
    cosine, sine = np.where(ok, cosine, 0.0), np.where(ok, sine, 0.0)
    z_forward = split_table(np.concatenate([cosine, sine], axis=1), 1)
    z_back = split_table(np.concatenate([cosine.T, -sine.T], axis=1), 1)

    y_of = np.array([s * YL + y for y in range(YL) for s in range(GY)])
    cosine, sine = wave(np.arange(NY), y_of, NY)
    y_forward = split_table(np.concatenate([cosine, sine], axis=1), 1)
    y_back = split_table(np.concatenate([cosine.T, -sine.T], axis=1), 1)
    return x_forward, z_forward, y_forward, y_back, z_back, x_back


def lane_ids(rows):
    return lax.broadcasted_iota(jnp.int32, (rows, 128), 1)


def block_swap(arrays):
    rows = next(a for a in arrays if a is not None).shape[0]
    lane = lane_ids(rows)
    arrays = [jnp.zeros((rows, 128), F32) if a is None else a for a in arrays]
    for step in (4, 2, 1):
        width = 16 * step
        low = (lane // width) % 2 == 0
        out = list(arrays)
        for i in range(8):
            if (i // step) % 2 == 0:
                a, b = arrays[i], arrays[i + step]
                out[i] = jnp.where(low, a, pltpu.roll(b, width, 1))
                out[i + step] = jnp.where(low, pltpu.roll(a, 128 - width, 1), b)
        arrays = out
    return arrays


def turned(x):
    real = (lane_ids(x.shape[0]) // 8) % 2 == 0
    return jnp.where(real, pltpu.roll(x, 120, 1), -pltpu.roll(x, 8, 1))


def halves(x):
    high = x.astype(BF16)
    return high, (x - high.astype(F32)).astype(BF16)


def put_operand(ref, row, count, lanes, x):
    high, low = halves(x)
    turn_high, turn_low = halves(turned(x))
    size = x.shape[0]
    for block, value in enumerate((high, turn_high, low, turn_low, high, turn_high)):
        ref[pl.ds(row + block * count, size), lanes] = value


def dot(a, b):
    return jnp.dot(a, b, preferred_element_type=F32)


def kernel(
    strain, phase, density, target, x_table, z_fwd_hbm, y_fwd_hbm, y_back_hbm, z_back_hbm, x_back_hbm,
    out,
    z_fwd, y_fwd, y_back, z_back, x_back,
    field, x_left, x_spec,
    f_send, f_recv, g_send, g_recv, h_send, h_recv, b_send, b_recv,
    z_right, y_right, y_spec, y_lines, back_left,
    table_sem, f_ssem, f_rsem, g_ssem, g_rsem, h_ssem, h_rsem, b_ssem, b_rsem,
):
    gy, gz = lax.axis_index("gy"), lax.axis_index("gz")

    loads = [
        pltpu.make_async_copy(src, dst, table_sem.at[i])
        for i, (src, dst) in enumerate(
            ((z_fwd_hbm, z_fwd), (y_fwd_hbm, y_fwd), (y_back_hbm, y_back), (z_back_hbm, z_back), (x_back_hbm, x_back))
        )
    ]
    for load in loads:
        load.start()

    f_recv[...] = jnp.zeros_like(f_recv)
    h_recv[...] = jnp.zeros_like(h_recv)

    barrier = pltpu.get_barrier_semaphore()

    def greet(axis, me, n):
        def body(i, carry):
            pl.semaphore_signal(barrier, inc=1, device_id={axis: lax.rem(me + i, n)}, device_id_type=MESH)
            return carry

        lax.fori_loop(1, n, body, 0)

    greet("gz", gz, GZ)
    greet("gy", gy, GY)

    def transfer(axis, me, n, pad, used, src, dst, ssem, rsem, chunk, tiles):
        lo, hi = tiles

        def copy(i):
            hop = lax.div(i + 1, 2)
            there = lax.rem(me + jnp.where(lax.rem(i, 2) == 1, hop, n - hop), n)
            return pltpu.make_async_remote_copy(
                src_ref=src.at[lo:hi, pl.ds(pl.multiple_of(there * pad, pad), used), :],
                dst_ref=dst.at[lo:hi, pl.ds(pl.multiple_of(me * pad, pad), used), :],
                send_sem=ssem.at[chunk, i],
                recv_sem=rsem.at[chunk, i],
                device_id={axis: there},
                device_id_type=MESH,
            )

        def start():
            lax.fori_loop(1, n, lambda i, c: (copy(i).start(), c)[1], 0)
            own = pl.ds(pl.multiple_of(me * pad, pad), used)
            dst[lo:hi, own, :] = src[lo:hi, own, :]

        def wait_recv():
            lax.fori_loop(1, n, lambda i, c: (copy(i).wait_recv(), c)[1], 0)

        def wait_send():
            lax.fori_loop(1, n, lambda i, c: (copy(i).wait_send(), c)[1], 0)

        return start, wait_recv, wait_send

    to_z = [transfer("gz", gz, GZ, 16, ZL, f_send, f_recv, f_ssem, f_rsem, h, FORWARD[h]) for h in range(2)]
    to_y = [transfer("gy", gy, GY, 8, 6, g_send, g_recv, g_ssem, g_rsem, h, FORWARD[h]) for h in range(2)]
    from_y = [transfer("gy", gy, GY, 8, 6, h_send, h_recv, h_ssem, h_rsem, h, BACKWARD[h]) for h in range(2)]
    from_z = [transfer("gz", gz, GZ, 16, ZL, b_send, b_recv, b_ssem, b_rsem, h, BACKWARD[h]) for h in range(2)]

    cubes = [density[i] * density[i] * density[i] for i in range(16)]
    least, most = cubes[0], cubes[0]
    for value in cubes[1:]:
        least, most = jnp.minimum(least, value), jnp.maximum(most, value)
    middle = 0.5 * (least + most)
    lame_ref, shear_ref = LAME_SOLID * middle, SHEAR_SOLID * middle

    field[...] = jnp.zeros_like(field)

    def polarize(y, carry):
        level = phase[y]
        stiff = jnp.zeros(level.shape, F32)
        for i, value in enumerate(cubes):
            stiff = jnp.where(level == i, value, stiff)
        excess = stiff - middle
        parts = [strain[c, y] for c in range(6)]
        trace = LAME_SOLID * (parts[0] + parts[1] + parts[2])
        for c in range(6):
            value = (2.0 * SHEAR_SOLID) * parts[c]
            field[c * YL + y, 0:ZL, :] = excess * (value + trace if c < 3 else value)
        return carry

    lax.fori_loop(0, YL, polarize, 0)

    def split_rows(g, carry):
        high, low = halves(field[g])
        rows = pl.ds(pl.multiple_of(g * 16, 16), 16)
        x_left[rows, 0:512] = high
        x_left[rows, 512:1024] = low
        x_left[rows, 1024:1536] = high
        return carry

    lax.fori_loop(0, 36, split_rows, 0)
    x_spec[...] = dot(x_left[...], x_table[...])

    def spread(h, tile, first):
        for half in range(2):
            lanes = slice((h * 2 + half) * 128, (h * 2 + half + 1) * 128)
            pieces = [x_spec[pl.ds(pl.multiple_of((first + j) * 16, 16), 16), lanes] for j in range(8)]
            for i, piece in enumerate(block_swap(pieces)):
                f_send[tile, (half * 8 + i) * 16 : (half * 8 + i + 1) * 16, :] = piece

    def spread_chunk(h):
        lax.fori_loop(0, 4, lambda t, c: (spread(h, h * 5 + t, t * 8), c)[1], 0)

    spread_chunk(0)
    for half in range(2):
        pieces = [
            x_spec[(32 + j % 4) * 16 : (33 + j % 4) * 16, ((j // 4) * 2 + half) * 128 : ((j // 4) * 2 + half + 1) * 128]
            for j in range(8)
        ]
        for i, piece in enumerate(block_swap(pieces)):
            f_send[4, (half * 8 + i) * 16 : (half * 8 + i + 1) * 16, :] = piece

    pl.semaphore_wait(barrier, GZ - 1 + GY - 1)
    to_z[0][0]()
    spread_chunk(1)
    to_z[1][0]()

    def z_transform(table, source, result, tiles):
        lo, hi = tiles

        def fill(i, carry):
            lanes = pl.ds(pl.multiple_of(i * 128, 128), 128)
            for part in range(4):
                put_operand(z_right, part * 64, 256, lanes, source[lo + i, part * 64 : (part + 1) * 64, :])
            return carry

        lax.fori_loop(0, hi - lo, fill, 0)
        value = dot(table[...], z_right[:, 0 : (hi - lo) * 128])
        for i in range(hi - lo):
            result[lo + i] = value[:, i * 128 : (i + 1) * 128]

    def tile_of(h, t):
        return 4 if t == 4 else h * 5 + t

    def y_transform(h):
        for t in range(5):
            pieces = [g_recv[tile_of(h, t), pl.ds(k, GY, stride=8), :] for k in range(6)] + [None, None]
            swapped = block_swap(pieces)
            for b in range(8) if t < 4 else range(4):
                g = t * 8 + b
                c, y = g // YL, g % YL
                piece = swapped[b] if t < 4 else swapped[h * 4 + b]
                put_operand(y_right, y * GY, NY, slice(c * 128, (c + 1) * 128), piece)
        y_spec[...] = dot(y_fwd[...], y_right[...])

    def green(h):
        rows = 16
        lane = lane_ids(1)
        k8, part, z8 = lane % 8, (lane // 8) % 2, lane // 16
        wave_x = gz * 16 + h * 8 + k8
        wave_z = gy * 6 + z8
        signed_z = jnp.where(wave_z > NZ // 2, wave_z - NZ, wave_z)
        fx = jnp.broadcast_to(wave_x.astype(F32) / NX, (rows, 128))
        fz = jnp.broadcast_to(signed_z.astype(F32) / NZ, (rows, 128))
        lane_ok = (z8 < 6) & (wave_z != NZ // 2)
        weight = jnp.where(lane_ok, jnp.where(wave_x == 0, -1.0 / VOXELS, -2.0 / VOXELS), 0.0)
        origin = (wave_x == 0) & (wave_z == 0) & (z8 < 6)
        coupling = (lame_ref + shear_ref) / (shear_ref * (lame_ref + 2.0 * shear_ref))
        half_shear = 1.0 / (2.0 * shear_ref)

        def body(step, carry):
            start = pl.multiple_of(step * rows, rows)
            wave_y = start + lax.broadcasted_iota(jnp.int32, (rows, 128), 0)
            fy = jnp.where(wave_y > NY // 2, wave_y - NY, wave_y).astype(F32) / NY
            zero = origin & (wave_y == 0)
            keep = (wave_y != NY // 2) & jnp.logical_not(zero)
            norm = jnp.where(zero, 1.0, fx * fx + fy * fy + fz * fz)
            inverse = 1.0 / norm
            scale = jnp.where(keep, weight * inverse, 0.0)
            s = [y_spec[pl.ds(start, rows), c * 128 : (c + 1) * 128] for c in range(6)]
            vector = [
                fx * s[0] + fy * s[5] + fz * s[4],
                fx * s[5] + fy * s[1] + fz * s[3],
                fx * s[4] + fy * s[3] + fz * s[2],
            ]
            projected = fx * vector[0] + fy * vector[1] + fz * vector[2]
            fourth = (0.5 * coupling) * projected * inverse
            frequency = (fx, fy, fz)
            move = [scale * (half_shear * vector[i] - frequency[i] * fourth) for i in range(3)]
            images = [2.0 * frequency[i] * move[i] for i in range(3)]
            images += [frequency[i] * move[j] + frequency[j] * move[i] for i, j in ((1, 2), (0, 2), (0, 1))]
            real = (part == 0).astype(F32)
            gap = [target[c] * real - s[c] * (1.0 / VOXELS) for c in range(6)]
            gap_trace = (gap[0] + gap[1] + gap[2]) * (lame_ref / (3.0 * lame_ref + 2.0 * shear_ref))
            for c in range(6):
                macro = (gap[c] - gap_trace if c < 3 else gap[c]) * half_shear
                put_operand(y_right, start, NY, slice(c * 128, (c + 1) * 128), jnp.where(zero, macro, images[c]))
            return carry

        lax.fori_loop(0, NY // rows, body, 0)

    def y_inverse(h):
        y_lines[h] = dot(y_back[...], y_right[...])
        for t in range(4) if h == 0 else range(5):
            pieces = []
            for b in range(8):
                g = t * 8 + b if t < 4 else 32 + b % 4
                c, y = g // YL, g % YL
                source = h if t < 4 else b // 4
                pieces.append(y_lines[source, y * GY : (y + 1) * GY, c * 128 : (c + 1) * 128])
            swapped = block_swap(pieces)
            for k in range(6):
                h_send[tile_of(h, t), pl.ds(k, GY, stride=8), :] = swapped[k]

    def gather_half(tile, g, half, b_range, h):
        pieces = [b_recv[tile, (half * 8 + i) * 16 : (half * 8 + i + 1) * 16, :] for i in range(8)]
        swapped = block_swap(pieces)
        for n, b in enumerate(b_range):
            high, low = halves(swapped[b])
            rows = pl.ds(pl.multiple_of((g + n) * 16, 16), 16)
            for block, value in enumerate((high, low, high)):
                back_left[h, rows, block * 256 + half * 128 : block * 256 + (half + 1) * 128] = value

    def gather(h):
        def body(t, carry):
            for half in range(2):
                gather_half(h * 5 + t, t * 8, half, range(8), h)
            return carry

        lax.fori_loop(0, 4, body, 0)

    for load in loads:
        load.wait()

    to_z[0][1]()
    z_transform(z_fwd, f_recv, g_send, FORWARD[0])
    to_y[0][0]()
    to_y[0][1]()
    y_transform(0)
    green(0)
    y_inverse(0)
    from_y[0][0]()

    to_z[1][1]()
    z_transform(z_fwd, f_recv, g_send, FORWARD[1])
    to_y[1][0]()

    from_y[0][1]()
    z_transform(z_back, h_recv, b_send, BACKWARD[0])
    from_z[0][0]()

    to_y[1][1]()
    y_transform(1)
    green(1)
    y_inverse(1)
    from_y[1][0]()

    from_y[1][1]()
    z_transform(z_back, h_recv, b_send, BACKWARD[1])
    from_z[1][0]()

    from_z[0][1]()
    gather(0)
    x_spec[0:512, :] = dot(back_left[0, 0:512, :], x_back[0])
    from_z[1][1]()
    gather(1)
    for half in range(2):
        for h in range(2):
            gather_half(4, 32, half, range(h * 4, h * 4 + 4), h)
    x_spec[512:576, :] = dot(back_left[0, 512:576, :], x_back[0])
    x_spec[...] += dot(back_left[1], x_back[1])
    for c in range(6):
        for y in range(YL):
            g = c * YL + y
            out[c, y] = x_spec[g * 16 : g * 16 + ZL, :]

    for group in (to_z, to_y, from_y, from_z):
        for h in range(2):
            group[h][2]()


def local(strain, phase, density, target):
    consts = [jnp.asarray(table) for table in tables()]
    vmem = pl.BlockSpec(memory_space=pltpu.VMEM)
    smem = pl.BlockSpec(memory_space=pltpu.SMEM)
    hbm = pl.BlockSpec(memory_space=pl.ANY)
    dma = pltpu.SemaphoreType.DMA
    return pl.pallas_call(
        kernel,
        out_shape=jax.ShapeDtypeStruct((6, YL, ZL, NX), F32),
        in_specs=[vmem, vmem, smem, smem, vmem] + [hbm] * 5,
        out_specs=vmem,
        scratch_shapes=[pltpu.VMEM(table.shape, BF16) for table in consts[1:]]
        + [
            pltpu.VMEM((36, 16, NX), F32),
            pltpu.VMEM((576, 3 * NX), BF16),
            pltpu.VMEM((576, NX), F32),
        ]
        + [pltpu.VMEM((TILES, 256, 128), F32)] * 8
        + [
            pltpu.VMEM((1536, 640), BF16),
            pltpu.VMEM((6 * NY, 768), BF16),
            pltpu.VMEM((NY, 768), F32),
            pltpu.VMEM((2, NY, 768), F32),
            pltpu.VMEM((2, 576, 768), BF16),
        ]
        + [dma((5,))]
        + [dma((2, GZ)), dma((2, GZ)), dma((2, GY)), dma((2, GY)), dma((2, GY)), dma((2, GY)), dma((2, GZ)), dma((2, GZ))],
        compiler_params=pltpu.CompilerParams(collective_id=0, has_side_effects=True, vmem_limit_bytes=56 * 2**20),
        cost_estimate=pl.CostEstimate(flops=3_500_000_000, bytes_accessed=8_000_000, transcendentals=0),
    )(strain, phase, density, target, *consts)


def solution(mesh):
    placed = (P(None, "gy", "gz", None), P("gy", "gz", None), P(), P())
    return jax.shard_map(local, mesh=mesh, in_specs=placed, out_specs=P(None, "gy", "gz", None), check_vma=False)
```

```python
import math

import jax
import jax.numpy as jnp
import ml_dtypes
import numpy as np
from jax import lax
from jax.experimental import pallas as pl
from jax.experimental.pallas import tpu as pltpu
from jax.sharding import PartitionSpec as P

NX, NY, NZ = 512, 192, 192
GY, GZ = 32, 16
YL, ZL = NY // GY, NZ // GZ
VOXELS = float(NX * NY * NZ)
LAME_SOLID = 0.5769230769
SHEAR_SOLID = 0.3846153846
MESH = pl.DeviceIdType.MESH
F32, BF16 = jnp.float32, jnp.bfloat16
TILES = 9
CHUNKS = 4
FORWARD = ((0, 3), (3, 5), (5, 7), (7, 9))
BACKWARD = ((0, 2), (2, 4), (4, 6), (6, 9))
SHARED_FORWARD, SHARED_BACK = 2, 8


def forward_tile(h, t):
    return t if h == 0 else 1 + 2 * h + t


def group_row(c2, m):
    return c2 * 2 + m - 16 if m >= 16 else 4 + c2 * 16 + m


def split_table(table, axis):
    high = table.astype(np.float32).astype(ml_dtypes.bfloat16)
    low = (table - high.astype(np.float64)).astype(np.float32).astype(ml_dtypes.bfloat16)
    return np.concatenate([high, high, low], axis=axis)


def wave(rows, columns, length):
    angle = 2.0 * math.pi / length * ((np.asarray(rows)[:, None] * np.asarray(columns)[None, :]) % length)
    return np.cos(angle), np.sin(angle)


def tables():
    kx = np.array([d * 16 + h * 4 + k for h in range(CHUNKS) for d in range(GZ) for _ in range(2) for k in range(4)])
    imag = np.array([r for _ in range(CHUNKS) for _ in range(GZ) for r in range(2) for _ in range(4)])
    cosine, sine = wave(np.arange(NX), kx, NX)
    x_table = np.where(imag[None, :] == 0, cosine, -sine)
    x_forward = split_table(x_table, 0)
    x_back = np.stack([split_table(x_table.T[h * 128 : (h + 1) * 128], 0) for h in range(CHUNKS)])

    z_rows = np.arange(GZ * 16)
    z_of, z_ok = (z_rows // 16) * ZL + np.minimum(z_rows % 16, ZL - 1), z_rows % 16 < ZL
    k_rows = np.arange(GY * 8)
    k_of, k_ok = (k_rows // 8) * 6 + np.minimum(k_rows % 8, 5), k_rows % 8 < 6
    cosine, sine = wave(k_of, z_of, NZ)
    ok = k_ok[:, None] & z_ok[None, :]
    cosine, sine = np.where(ok, cosine, 0.0), np.where(ok, sine, 0.0)
    z_forward = split_table(np.concatenate([cosine, sine], axis=1), 1)
    z_back = split_table(np.concatenate([cosine.T, -sine.T], axis=1), 1)

    y_of = np.array([s * YL + y for y in range(YL) for s in range(GY)])
    cosine, sine = wave(np.arange(NY), y_of, NY)
    y_forward = split_table(np.concatenate([cosine, sine], axis=1), 1)
    y_back = split_table(np.concatenate([cosine.T, -sine.T], axis=1), 1)
    return x_forward, z_forward, y_forward, y_back, z_back, x_back


def lane_ids(rows):
    return lax.broadcasted_iota(jnp.int32, (rows, 128), 1)


def block_swap(arrays, width=8):
    lane = lane_ids(arrays[0].shape[0])
    step = len(arrays) // 2
    while step:
        shift = width * step
        low = (lane // shift) % 2 == 0
        out = list(arrays)
        for i in range(len(arrays)):
            if (i // step) % 2 == 0:
                a, b = arrays[i], arrays[i + step]
                out[i] = jnp.where(low, a, pltpu.roll(b, shift, 1))
                out[i + step] = jnp.where(low, pltpu.roll(a, 128 - shift, 1), b)
        arrays, step = out, step // 2
    return arrays


def pair_swap(a, b):
    low = lane_ids(a.shape[0]) < 64
    return jnp.where(low, a, pltpu.roll(b, 64, 1)), jnp.where(low, pltpu.roll(a, 64, 1), b)


def turned(x):
    real = (lane_ids(x.shape[0]) // 4) % 2 == 0
    return jnp.where(real, pltpu.roll(x, 124, 1), -pltpu.roll(x, 4, 1))


def halves(x):
    high = x.astype(BF16)
    return high, (x - high.astype(F32)).astype(BF16)


def put_operand(ref, row, count, lanes, x):
    high, low = halves(x)
    turn_high, turn_low = halves(turned(x))
    size = x.shape[0]
    for block, value in enumerate((high, turn_high, low, turn_low)):
        ref[pl.ds(row + block * count, size), lanes] = value


def dot(a, b):
    return jnp.dot(a, b, preferred_element_type=F32)


def dot_right(table, ref, lanes):
    cut = ref.shape[0]
    return dot(table[:, 0:cut], ref[:, lanes]) + dot(table[:, cut:], ref[0 : cut // 2, lanes])


def dot_left(left, table, lanes):
    cut = left.shape[1]
    return dot(left, table[0:cut, lanes]) + dot(left[:, 0 : cut // 2], table[cut:, lanes])


def kernel(
    strain, phase, density, target, x_table_hbm, z_fwd_hbm, y_fwd_hbm, y_back_hbm, z_back_hbm, x_back_hbm,
    out,
    x_table, z_fwd, y_fwd, y_back, z_back, x_back,
    field, x_left, x_spec,
    f_send, f_recv, g_send, g_recv, h_send, h_recv, b_send, b_recv,
    z_right, y_right, y_spec, y_lines, back_left,
    table_sem, f_ssem, f_rsem, g_ssem, g_rsem, h_ssem, h_rsem, b_ssem, b_rsem,
):
    gy, gz = lax.axis_index("gy"), lax.axis_index("gz")

    loads = [
        pltpu.make_async_copy(src, dst, table_sem.at[i])
        for i, (src, dst) in enumerate(
            ((x_table_hbm, x_table), (z_fwd_hbm, z_fwd), (y_fwd_hbm, y_fwd), (y_back_hbm, y_back), (z_back_hbm, z_back), (x_back_hbm, x_back))
        )
    ]
    for load in loads:
        load.start()

    f_recv[...] = jnp.zeros_like(f_recv)
    h_recv[...] = jnp.zeros_like(h_recv)

    barrier = pltpu.get_barrier_semaphore()

    def greet(axis, me, n):
        def body(i, carry):
            pl.semaphore_signal(barrier, inc=1, device_id={axis: lax.rem(me + i, n)}, device_id_type=MESH)
            return carry

        lax.fori_loop(1, n, body, 0)

    greet("gz", gz, GZ)
    greet("gy", gy, GY)

    def transfer(axis, me, n, pad, used, src, dst, ssem, rsem, chunk, tiles):
        lo, hi = tiles

        def copy(i):
            hop = lax.div(i + 1, 2)
            there = lax.rem(me + jnp.where(lax.rem(i, 2) == 1, hop, n - hop), n)
            return pltpu.make_async_remote_copy(
                src_ref=src.at[lo:hi, pl.ds(pl.multiple_of(there * pad, pad), used), :],
                dst_ref=dst.at[lo:hi, pl.ds(pl.multiple_of(me * pad, pad), used), :],
                send_sem=ssem.at[chunk, i],
                recv_sem=rsem.at[chunk, i],
                device_id={axis: there},
                device_id_type=MESH,
            )

        def start():
            lax.fori_loop(1, n, lambda i, c: (copy(i).start(), c)[1], 0)
            own = pl.ds(pl.multiple_of(me * pad, pad), used)
            dst[lo:hi, own, :] = src[lo:hi, own, :]

        def wait_recv():
            lax.fori_loop(1, n, lambda i, c: (copy(i).wait_recv(), c)[1], 0)

        def wait_send():
            lax.fori_loop(1, n, lambda i, c: (copy(i).wait_send(), c)[1], 0)

        return start, wait_recv, wait_send

    to_z = [transfer("gz", gz, GZ, 16, ZL, f_send, f_recv, f_ssem, f_rsem, h, FORWARD[h]) for h in range(CHUNKS)]
    to_y = [transfer("gy", gy, GY, 8, 6, g_send, g_recv, g_ssem, g_rsem, h, FORWARD[h]) for h in range(CHUNKS)]
    from_y = [transfer("gy", gy, GY, 8, 6, h_send, h_recv, h_ssem, h_rsem, h, BACKWARD[h]) for h in range(CHUNKS)]
    from_z = [transfer("gz", gz, GZ, 16, ZL, b_send, b_recv, b_ssem, b_rsem, h, BACKWARD[h]) for h in range(CHUNKS)]

    cubes = [density[i] * density[i] * density[i] for i in range(16)]
    least, most = cubes[0], cubes[0]
    for value in cubes[1:]:
        least, most = jnp.minimum(least, value), jnp.maximum(most, value)
    middle = 0.5 * (least + most)
    lame_ref, shear_ref = LAME_SOLID * middle, SHEAR_SOLID * middle

    field[...] = jnp.zeros_like(field)

    def polarize(y, carry):
        level = phase[y]
        stiff = jnp.zeros(level.shape, F32)
        for i, value in enumerate(cubes):
            stiff = jnp.where(level == i, value, stiff)
        excess = stiff - middle
        parts = [strain[c, y] for c in range(6)]
        trace = LAME_SOLID * (parts[0] + parts[1] + parts[2])
        for c in range(6):
            value = (2.0 * SHEAR_SOLID) * parts[c]
            m = (c // 2) * YL + y
            row = jnp.where(m >= 16, c % 2 * 2 + m - 16, 4 + c % 2 * 16 + m)
            field[row, 0:ZL, :] = excess * (value + trace if c < 3 else value)
        return carry

    lax.fori_loop(0, YL, polarize, 0)

    def split_rows(g, carry):
        high, low = halves(field[g])
        rows = pl.ds(pl.multiple_of(g * 16, 16), 16)
        x_left[rows, 0:512] = high
        x_left[rows, 512:1024] = low
        return carry

    lax.fori_loop(0, 36, split_rows, 0)

    def x_transform(rows, lanes):
        x_spec[rows, lanes] = dot_left(x_left[rows, :], x_table, lanes)

    def x_piece(c2, m, h):
        row = group_row(c2, m) * 16
        return x_spec[row : row + 16, h * 128 : (h + 1) * 128]

    def send_tile(tile, pieces):
        for i, piece in enumerate(block_swap(pieces)):
            f_send[tile, i * 16 : (i + 1) * 16, :] = piece

    def spread(h):
        for t in range(2):
            send_tile(forward_tile(h, t), [x_piece(c2, t * 8 + b, h) for c2 in range(2) for b in range(8)])

    loads[0].wait()
    x_transform(slice(0, 576), slice(0, 128))
    x_transform(slice(0, 64), slice(128, 512))
    spread(0)
    send_tile(SHARED_FORWARD, [x_piece(c2, 16 + e, h) for c2 in range(2) for h in range(CHUNKS) for e in range(2)])
    pl.semaphore_wait(barrier, GZ - 1 + GY - 1)
    to_z[0][0]()
    for h in range(1, CHUNKS):
        x_transform(slice(64, 576), slice(h * 128, (h + 1) * 128))
        spread(h)
        to_z[h][0]()

    def z_transform(table, source, result, tiles):
        lo, hi = tiles

        def fill(i, carry):
            lanes = pl.ds(pl.multiple_of(i * 128, 128), 128)
            for part in range(4):
                put_operand(z_right, part * 64, 256, lanes, source[lo + i, part * 64 : (part + 1) * 64, :])
            return carry

        lax.fori_loop(0, hi - lo, fill, 0)
        value = dot_right(table, z_right, slice(0, (hi - lo) * 128))
        for i in range(hi - lo):
            result[lo + i] = value[:, i * 128 : (i + 1) * 128]

    def y_transform(h):
        def unpack(tile):
            pieces = [g_recv[tile, pl.ds(k, GY, stride=8), :] for k in range(6)]
            return block_swap(pieces + [jnp.zeros((GY, 128), F32)] * 2)

        for t in range(3):
            swapped = unpack(forward_tile(h, t)) if t < 2 else unpack(SHARED_FORWARD)[h * 2 : h * 2 + 2]
            for b, piece in enumerate(swapped):
                cp, y = (t * 8 + b) // YL, (t * 8 + b) % YL
                put_operand(y_right, y * GY, NY, slice(cp * 128, (cp + 1) * 128), piece)
        y_spec[...] = dot_right(y_fwd, y_right, slice(0, 384))

    def green(h):
        rows = 16
        lane = lane_ids(1)
        k4, part, z8 = lane % 4, (lane // 4) % 2, (lane // 8) % 8
        wave_x = gz * 16 + h * 4 + k4
        wave_z = gy * 6 + z8
        signed_z = jnp.where(wave_z > NZ // 2, wave_z - NZ, wave_z)
        fx = jnp.broadcast_to(wave_x.astype(F32) / NX, (rows, 128))
        fz = jnp.broadcast_to(signed_z.astype(F32) / NZ, (rows, 128))
        lane_ok = (z8 < 6) & (wave_z != NZ // 2)
        weight = jnp.where(lane_ok, jnp.where(wave_x == 0, -1.0 / VOXELS, -2.0 / VOXELS), 0.0)
        origin = (wave_x == 0) & (wave_z == 0) & (z8 < 6)
        coupling = (lame_ref + shear_ref) / (shear_ref * (lame_ref + 2.0 * shear_ref))
        half_shear = 1.0 / (2.0 * shear_ref)

        def body(step, carry):
            start = pl.multiple_of(step * rows, rows)
            upper = pl.multiple_of(start + NY // 2, rows)
            wave_y = start + lax.broadcasted_iota(jnp.int32, (rows, 128), 0)
            wave_y = wave_y + jnp.where(lane_ids(rows) < 64, 0, NY // 2)
            fy = jnp.where(wave_y > NY // 2, wave_y - NY, wave_y).astype(F32) / NY
            zero = origin & (wave_y == 0)
            keep = (wave_y != NY // 2) & jnp.logical_not(zero)
            norm = jnp.where(zero, 1.0, fx * fx + fy * fy + fz * fz)
            inverse = 1.0 / norm
            scale = jnp.where(keep, weight * inverse, 0.0)
            s = []
            for cp in range(3):
                lanes = slice(cp * 128, (cp + 1) * 128)
                s += pair_swap(y_spec[pl.ds(start, rows), lanes], y_spec[pl.ds(upper, rows), lanes])
            vector = [
                fx * s[0] + fy * s[5] + fz * s[4],
                fx * s[5] + fy * s[1] + fz * s[3],
                fx * s[4] + fy * s[3] + fz * s[2],
            ]
            projected = fx * vector[0] + fy * vector[1] + fz * vector[2]
            fourth = (0.5 * coupling) * projected * inverse
            frequency = (fx, fy, fz)
            move = [scale * (half_shear * vector[i] - frequency[i] * fourth) for i in range(3)]
            images = [2.0 * frequency[i] * move[i] for i in range(3)]
            images += [frequency[i] * move[j] + frequency[j] * move[i] for i, j in ((1, 2), (0, 2), (0, 1))]
            real = (part == 0).astype(F32)
            gap = [target[c] * real - s[c] * (1.0 / VOXELS) for c in range(6)]
            gap_trace = (gap[0] + gap[1] + gap[2]) * (lame_ref / (3.0 * lame_ref + 2.0 * shear_ref))
            for c in range(6):
                macro = (gap[c] - gap_trace if c < 3 else gap[c]) * half_shear
                images[c] = jnp.where(zero, macro, images[c])
            for cp in range(3):
                lanes = slice(cp * 128, (cp + 1) * 128)
                first, second = pair_swap(images[2 * cp], images[2 * cp + 1])
                put_operand(y_right, start, NY, lanes, first)
                put_operand(y_right, upper, NY, lanes, second)
            return carry

        lax.fori_loop(0, NY // 2 // rows, body, 0)

    def y_inverse(h):
        y_lines[h] = dot_right(y_back, y_right, slice(0, 384))

        def line(chunk, m):
            cp, y = m // YL, m % YL
            return y_lines[chunk, y * GY : (y + 1) * GY, cp * 128 : (cp + 1) * 128]

        def pack(tile, pieces):
            swapped = block_swap(pieces)
            for k in range(6):
                h_send[tile, pl.ds(k, GY, stride=8), :] = swapped[k]

        for t in range(2):
            pack(2 * h + t, [line(h, t * 8 + b) for b in range(8)])
        if h == CHUNKS - 1:
            pack(SHARED_BACK, [line(chunk, 16 + e) for chunk in range(CHUNKS) for e in range(2)])

    def gather(tile, places):
        swapped = block_swap([b_recv[tile, i * 16 : (i + 1) * 16, :] for i in range(GZ)])
        for (h, row), piece in zip(places, swapped, strict=True):
            high, low = halves(piece)
            back_left[h, row * 16 : (row + 1) * 16, 0:128] = high
            back_left[h, row * 16 : (row + 1) * 16, 128:256] = low

    def x_inverse(h):
        for t in range(2):
            gather(2 * h + t, [(h, group_row(c2, t * 8 + b)) for c2 in range(2) for b in range(8)])
        value = dot_left(back_left[h, 64:576, :], x_back.at[h], slice(0, NX))
        x_spec[64:576, :] = value if h == 0 else x_spec[64:576, :] + value

    def x_shared():
        gather(
            SHARED_BACK,
            [(h, group_row(c2, 16 + e)) for c2 in range(2) for h in range(CHUNKS) for e in range(2)],
        )
        x_spec[0:64, :] = sum(dot_left(back_left[h, 0:64, :], x_back.at[h], slice(0, NX)) for h in range(CHUNKS))

    for load in loads[1:]:
        load.wait()

    def stage_z(h):
        to_z[h][1]()
        z_transform(z_fwd, f_recv, g_send, FORWARD[h])
        to_y[h][0]()

    def stage_y(h):
        to_y[h][1]()
        y_transform(h)
        green(h)
        y_inverse(h)
        from_y[h][0]()

    def stage_back(h):
        from_y[h][1]()
        z_transform(z_back, h_recv, b_send, BACKWARD[h])
        from_z[h][0]()

    def stage_x(h):
        from_z[h][1]()
        x_inverse(h)

    stage_z(0)
    stage_z(1)
    stage_y(0)
    stage_z(2)
    stage_y(1)
    stage_back(0)
    stage_z(3)
    stage_y(2)
    stage_back(1)
    stage_y(3)
    stage_back(2)
    stage_x(0)
    stage_back(3)
    stage_x(1)
    stage_x(2)
    for group in (to_z, to_y, from_y, from_z):
        for h in range(CHUNKS - (group is from_z)):
            group[h][2]()
    stage_x(3)
    x_shared()
    for c in range(6):
        for y in range(YL):
            row = group_row(c % 2, c // 2 * YL + y) * 16
            out[c, y] = x_spec[row : row + ZL, :]
    from_z[CHUNKS - 1][2]()


def local(strain, phase, density, target):
    consts = [jnp.asarray(table) for table in tables()]
    vmem = pl.BlockSpec(memory_space=pltpu.VMEM)
    smem = pl.BlockSpec(memory_space=pltpu.SMEM)
    hbm = pl.BlockSpec(memory_space=pl.ANY)
    dma = pltpu.SemaphoreType.DMA
    return pl.pallas_call(
        kernel,
        out_shape=jax.ShapeDtypeStruct((6, YL, ZL, NX), F32),
        in_specs=[vmem, vmem, smem, smem] + [hbm] * 6,
        out_specs=vmem,
        scratch_shapes=[pltpu.VMEM(table.shape, BF16) for table in consts]
        + [
            pltpu.VMEM((36, 16, NX), F32),
            pltpu.VMEM((576, 2 * NX), BF16),
            pltpu.VMEM((576, NX), F32),
        ]
        + [pltpu.VMEM((TILES, 256, 128), F32)] * 8
        + [
            pltpu.VMEM((1024, 384), BF16),
            pltpu.VMEM((4 * NY, 384), BF16),
            pltpu.VMEM((NY, 384), F32),
            pltpu.VMEM((CHUNKS, NY, 384), F32),
            pltpu.VMEM((CHUNKS, 576, 256), BF16),
        ]
        + [dma((6,))]
        + [dma((CHUNKS, n)) for n in (GZ, GZ, GY, GY, GY, GY, GZ, GZ)],
        compiler_params=pltpu.CompilerParams(collective_id=0, has_side_effects=True, vmem_limit_bytes=56 * 2**20),
        cost_estimate=pl.CostEstimate(flops=3_500_000_000, bytes_accessed=8_000_000, transcendentals=0),
    )(strain, phase, density, target, *consts)


def solution(mesh):
    placed = (P(None, "gy", "gz", None), P("gy", "gz", None), P(), P())
    return jax.shard_map(local, mesh=mesh, in_specs=placed, out_specs=P(None, "gy", "gz", None), check_vma=False)
```

```python
import math

import jax
import jax.numpy as jnp
import ml_dtypes
import numpy as np
from jax import lax
from jax.experimental import pallas as pl
from jax.experimental.pallas import tpu as pltpu
from jax.sharding import PartitionSpec as P

NX, NY, NZ = 512, 192, 192
GY, GZ = 32, 16
YL, ZL = NY // GY, NZ // GZ
VOXELS = float(NX * NY * NZ)
LAME_SOLID = 0.5769230769
SHEAR_SOLID = 0.3846153846
MESH = pl.DeviceIdType.MESH
F32, BF16 = jnp.float32, jnp.bfloat16
TILES = 9
CHUNKS = 4
FORWARD = ((0, 3), (3, 5), (5, 7), (7, 9))
BACKWARD = ((0, 2), (2, 4), (4, 6), (6, 9))
SHARED_FORWARD, SHARED_BACK = 2, 8


def forward_tile(h, t):
    return t if h == 0 else 1 + 2 * h + t


def group_row(c2, m):
    return c2 * 2 + m - 16 if m >= 16 else 4 + c2 * 16 + m


def split_table(table, axis):
    high = table.astype(np.float32).astype(ml_dtypes.bfloat16)
    low = (table - high.astype(np.float64)).astype(np.float32).astype(ml_dtypes.bfloat16)
    return np.concatenate([high, high, low], axis=axis)


def wave(rows, columns, length):
    angle = 2.0 * math.pi / length * ((np.asarray(rows)[:, None] * np.asarray(columns)[None, :]) % length)
    return np.cos(angle), np.sin(angle)


def tables():
    kx = np.array([d * 16 + h * 4 + k for h in range(CHUNKS) for d in range(GZ) for _ in range(2) for k in range(4)])
    imag = np.array([r for _ in range(CHUNKS) for _ in range(GZ) for r in range(2) for _ in range(4)])
    cosine, sine = wave(np.arange(NX), kx, NX)
    x_table = np.where(imag[None, :] == 0, cosine, -sine)
    x_forward = split_table(x_table, 0)
    x_back = np.stack([split_table(x_table.T[h * 128 : (h + 1) * 128], 0) for h in range(CHUNKS)])

    z_rows = np.arange(GZ * 16)
    z_of, z_ok = (z_rows // 16) * ZL + np.minimum(z_rows % 16, ZL - 1), z_rows % 16 < ZL
    k_rows = np.arange(GY * 8)
    k_of, k_ok = (k_rows // 8) * 6 + np.minimum(k_rows % 8, 5), k_rows % 8 < 6
    cosine, sine = wave(k_of, z_of, NZ)
    ok = k_ok[:, None] & z_ok[None, :]
    cosine, sine = np.where(ok, cosine, 0.0), np.where(ok, sine, 0.0)
    z_forward = split_table(np.concatenate([cosine, sine], axis=1), 1)
    z_back = split_table(np.concatenate([cosine.T, -sine.T], axis=1), 1)

    y_of = np.array([s * YL + y for y in range(YL) for s in range(GY)])
    cosine, sine = wave(np.arange(NY), y_of, NY)
    y_forward = split_table(np.concatenate([cosine, sine], axis=1), 1)
    y_back = split_table(np.concatenate([cosine.T, -sine.T], axis=1), 1)
    return x_forward, z_forward, y_forward, y_back, z_back, x_back


def lane_ids(rows):
    return lax.broadcasted_iota(jnp.int32, (rows, 128), 1)


def block_swap(arrays, width=8):
    lane = lane_ids(arrays[0].shape[0])
    step = len(arrays) // 2
    while step:
        shift = width * step
        low = (lane // shift) % 2 == 0
        out = list(arrays)
        for i in range(len(arrays)):
            if (i // step) % 2 == 0:
                a, b = arrays[i], arrays[i + step]
                out[i] = jnp.where(low, a, pltpu.roll(b, shift, 1))
                out[i + step] = jnp.where(low, pltpu.roll(a, 128 - shift, 1), b)
        arrays, step = out, step // 2
    return arrays


def pair_swap(a, b):
    low = lane_ids(a.shape[0]) < 64
    return jnp.where(low, a, pltpu.roll(b, 64, 1)), jnp.where(low, pltpu.roll(a, 64, 1), b)


def turned(x):
    real = (lane_ids(x.shape[0]) // 4) % 2 == 0
    return jnp.where(real, pltpu.roll(x, 124, 1), -pltpu.roll(x, 4, 1))


def halves(x):
    high = x.astype(BF16)
    return high, (x - high.astype(F32)).astype(BF16)


def put_operand(ref, row, count, lanes, x):
    high, low = halves(x)
    turn_high, turn_low = halves(turned(x))
    size = x.shape[0]
    for block, value in enumerate((high, turn_high, low, turn_low)):
        ref[pl.ds(row + block * count, size), lanes] = value


def dot(a, b):
    return jnp.dot(a, b, preferred_element_type=F32)


def dot_right(table, ref, lanes):
    cut = ref.shape[0]
    return dot(table[:, 0:cut], ref[:, lanes]) + dot(table[:, cut:], ref[0 : cut // 2, lanes])


def dot_left(left, table, lanes):
    cut = left.shape[1]
    return dot(left, table[0:cut, lanes]) + dot(left[:, 0 : cut // 2], table[cut:, lanes])


def kernel(
    strain, phase, density, target, x_table_hbm, z_fwd_hbm, y_fwd_hbm, y_back_hbm, z_back_hbm, x_back_hbm,
    out,
    x_table, z_fwd, y_fwd, y_back, z_back, x_back,
    field, x_left, x_spec,
    f_send, f_recv, g_send, g_recv, h_send, h_recv, b_send, b_recv,
    z_right, y_right, y_spec, y_lines, back_left,
    table_sem, f_ssem, f_rsem, g_ssem, g_rsem, h_ssem, h_rsem, b_ssem, b_rsem,
):
    gy, gz = lax.axis_index("gy"), lax.axis_index("gz")

    loads = [
        pltpu.make_async_copy(src, dst, table_sem.at[i])
        for i, (src, dst) in enumerate(
            ((x_table_hbm, x_table), (z_fwd_hbm, z_fwd), (y_fwd_hbm, y_fwd), (y_back_hbm, y_back), (z_back_hbm, z_back), (x_back_hbm, x_back))
        )
    ]
    for load in loads:
        load.start()

    f_recv[...] = jnp.zeros_like(f_recv)
    h_recv[...] = jnp.zeros_like(h_recv)

    barrier = pltpu.get_barrier_semaphore()

    def greet(axis, me, n):
        def body(i, carry):
            pl.semaphore_signal(barrier, inc=1, device_id={axis: lax.rem(me + i, n)}, device_id_type=MESH)
            return carry

        lax.fori_loop(1, n, body, 0)

    greet("gz", gz, GZ)
    greet("gy", gy, GY)

    def transfer(axis, me, n, pad, used, src, dst, ssem, rsem, chunk, tiles):
        lo, hi = tiles

        def copy(i):
            hop = n // 2 - lax.div(i, 2)
            there = lax.rem(me + jnp.where(lax.rem(i, 2) == 1, hop, n - hop), n)
            return pltpu.make_async_remote_copy(
                src_ref=src.at[lo:hi, pl.ds(pl.multiple_of(there * pad, pad), used), :],
                dst_ref=dst.at[lo:hi, pl.ds(pl.multiple_of(me * pad, pad), used), :],
                send_sem=ssem.at[chunk],
                recv_sem=rsem.at[chunk],
                device_id={axis: there},
                device_id_type=MESH,
            )

        def start():
            lax.fori_loop(1, n, lambda i, c: (copy(i).start(), c)[1], 0)
            own = pl.ds(pl.multiple_of(me * pad, pad), used)
            dst[lo:hi, own, :] = src[lo:hi, own, :]

        def all_copies():
            rows = (n - 1) * used
            return pltpu.make_async_remote_copy(
                src_ref=src.at[lo:hi, 0:rows, :],
                dst_ref=dst.at[lo:hi, 0:rows, :],
                send_sem=ssem.at[chunk],
                recv_sem=rsem.at[chunk],
                device_id={axis: lax.rem(me + 1, n)},
                device_id_type=MESH,
            )

        def wait_recv():
            all_copies().wait_recv()

        def wait_send():
            all_copies().wait_send()

        return start, wait_recv, wait_send

    to_z = [transfer("gz", gz, GZ, 16, ZL, f_send, f_recv, f_ssem, f_rsem, h, FORWARD[h]) for h in range(CHUNKS)]
    to_y = [transfer("gy", gy, GY, 8, 6, g_send, g_recv, g_ssem, g_rsem, h, FORWARD[h]) for h in range(CHUNKS)]
    from_y = [transfer("gy", gy, GY, 8, 6, h_send, h_recv, h_ssem, h_rsem, h, BACKWARD[h]) for h in range(CHUNKS)]
    from_z = [transfer("gz", gz, GZ, 16, ZL, b_send, b_recv, b_ssem, b_rsem, h, BACKWARD[h]) for h in range(CHUNKS)]

    cubes = [density[i] * density[i] * density[i] for i in range(16)]
    least, most = cubes[0], cubes[0]
    for value in cubes[1:]:
        least, most = jnp.minimum(least, value), jnp.maximum(most, value)
    middle = 0.5 * (least + most)
    lame_ref, shear_ref = LAME_SOLID * middle, SHEAR_SOLID * middle

    field[...] = jnp.zeros_like(field)

    def polarize(y, carry):
        level = phase[y]
        stiff = jnp.zeros(level.shape, F32)
        for i, value in enumerate(cubes):
            stiff = jnp.where(level == i, value, stiff)
        excess = stiff - middle
        parts = [strain[c, y] for c in range(6)]
        trace = LAME_SOLID * (parts[0] + parts[1] + parts[2])
        for c in range(6):
            value = (2.0 * SHEAR_SOLID) * parts[c]
            m = (c // 2) * YL + y
            row = jnp.where(m >= 16, c % 2 * 2 + m - 16, 4 + c % 2 * 16 + m)
            field[row, 0:ZL, :] = excess * (value + trace if c < 3 else value)
        return carry

    lax.fori_loop(0, YL, polarize, 0)

    def split_rows(g, carry):
        high, low = halves(field[g])
        rows = pl.ds(pl.multiple_of(g * 16, 16), 16)
        x_left[rows, 0:512] = high
        x_left[rows, 512:1024] = low
        return carry

    lax.fori_loop(0, 36, split_rows, 0)

    def x_transform(rows, lanes):
        x_spec[rows, lanes] = dot_left(x_left[rows, :], x_table, lanes)

    def x_piece(c2, m, h):
        row = group_row(c2, m) * 16
        return x_spec[row : row + 16, h * 128 : (h + 1) * 128]

    def send_tile(tile, pieces):
        for i, piece in enumerate(block_swap(pieces)):
            f_send[tile, i * 16 : (i + 1) * 16, :] = piece

    def spread(h):
        for t in range(2):
            send_tile(forward_tile(h, t), [x_piece(c2, t * 8 + b, h) for c2 in range(2) for b in range(8)])

    loads[0].wait()
    x_transform(slice(0, 576), slice(0, 128))
    x_transform(slice(0, 64), slice(128, 512))
    spread(0)
    send_tile(SHARED_FORWARD, [x_piece(c2, 16 + e, h) for c2 in range(2) for h in range(CHUNKS) for e in range(2)])
    pl.semaphore_wait(barrier, GZ - 1 + GY - 1)
    to_z[0][0]()
    for h in range(1, CHUNKS):
        x_transform(slice(64, 576), slice(h * 128, (h + 1) * 128))
        spread(h)
        to_z[h][0]()

    def z_transform(table, source, result, tiles):
        lo, hi = tiles

        def fill(i, carry):
            lanes = pl.ds(pl.multiple_of(i * 128, 128), 128)
            for part in range(4):
                put_operand(z_right, part * 64, 256, lanes, source[lo + i, part * 64 : (part + 1) * 64, :])
            return carry

        lax.fori_loop(0, hi - lo, fill, 0)
        value = dot_right(table, z_right, slice(0, (hi - lo) * 128))
        for i in range(hi - lo):
            result[lo + i] = value[:, i * 128 : (i + 1) * 128]

    def y_transform(h):
        def unpack(tile):
            pieces = [g_recv[tile, pl.ds(k, GY, stride=8), :] for k in range(6)]
            return block_swap(pieces + [jnp.zeros((GY, 128), F32)] * 2)

        for t in range(3):
            swapped = unpack(forward_tile(h, t)) if t < 2 else unpack(SHARED_FORWARD)[h * 2 : h * 2 + 2]
            for b, piece in enumerate(swapped):
                cp, y = (t * 8 + b) // YL, (t * 8 + b) % YL
                put_operand(y_right, y * GY, NY, slice(cp * 128, (cp + 1) * 128), piece)
        y_spec[...] = dot_right(y_fwd, y_right, slice(0, 384))

    def green(h):
        rows = 16
        lane = lane_ids(1)
        k4, part, z8 = lane % 4, (lane // 4) % 2, (lane // 8) % 8
        wave_x = gz * 16 + h * 4 + k4
        wave_z = gy * 6 + z8
        signed_z = jnp.where(wave_z > NZ // 2, wave_z - NZ, wave_z)
        fx = jnp.broadcast_to(wave_x.astype(F32) / NX, (rows, 128))
        fz = jnp.broadcast_to(signed_z.astype(F32) / NZ, (rows, 128))
        lane_ok = (z8 < 6) & (wave_z != NZ // 2)
        weight = jnp.where(lane_ok, jnp.where(wave_x == 0, -1.0 / VOXELS, -2.0 / VOXELS), 0.0)
        origin = (wave_x == 0) & (wave_z == 0) & (z8 < 6)
        coupling = (lame_ref + shear_ref) / (shear_ref * (lame_ref + 2.0 * shear_ref))
        half_shear = 1.0 / (2.0 * shear_ref)

        def body(step, carry):
            start = pl.multiple_of(step * rows, rows)
            upper = pl.multiple_of(start + NY // 2, rows)
            wave_y = start + lax.broadcasted_iota(jnp.int32, (rows, 128), 0)
            wave_y = wave_y + jnp.where(lane_ids(rows) < 64, 0, NY // 2)
            fy = jnp.where(wave_y > NY // 2, wave_y - NY, wave_y).astype(F32) / NY
            zero = origin & (wave_y == 0)
            keep = (wave_y != NY // 2) & jnp.logical_not(zero)
            norm = jnp.where(zero, 1.0, fx * fx + fy * fy + fz * fz)
            inverse = 1.0 / norm
            scale = jnp.where(keep, weight * inverse, 0.0)
            s = []
            for cp in range(3):
                lanes = slice(cp * 128, (cp + 1) * 128)
                s += pair_swap(y_spec[pl.ds(start, rows), lanes], y_spec[pl.ds(upper, rows), lanes])
            vector = [
                fx * s[0] + fy * s[5] + fz * s[4],
                fx * s[5] + fy * s[1] + fz * s[3],
                fx * s[4] + fy * s[3] + fz * s[2],
            ]
            projected = fx * vector[0] + fy * vector[1] + fz * vector[2]
            fourth = (0.5 * coupling) * projected * inverse
            frequency = (fx, fy, fz)
            move = [scale * (half_shear * vector[i] - frequency[i] * fourth) for i in range(3)]
            images = [2.0 * frequency[i] * move[i] for i in range(3)]
            images += [frequency[i] * move[j] + frequency[j] * move[i] for i, j in ((1, 2), (0, 2), (0, 1))]
            real = (part == 0).astype(F32)
            gap = [target[c] * real - s[c] * (1.0 / VOXELS) for c in range(6)]
            gap_trace = (gap[0] + gap[1] + gap[2]) * (lame_ref / (3.0 * lame_ref + 2.0 * shear_ref))
            for c in range(6):
                macro = (gap[c] - gap_trace if c < 3 else gap[c]) * half_shear
                images[c] = jnp.where(zero, macro, images[c])
            for cp in range(3):
                lanes = slice(cp * 128, (cp + 1) * 128)
                first, second = pair_swap(images[2 * cp], images[2 * cp + 1])
                put_operand(y_right, start, NY, lanes, first)
                put_operand(y_right, upper, NY, lanes, second)
            return carry

        lax.fori_loop(0, NY // 2 // rows, body, 0)

    def y_inverse(h):
        y_lines[h] = dot_right(y_back, y_right, slice(0, 384))

        def line(chunk, m):
            cp, y = m // YL, m % YL
            return y_lines[chunk, y * GY : (y + 1) * GY, cp * 128 : (cp + 1) * 128]

        def pack(tile, pieces):
            swapped = block_swap(pieces)
            for k in range(6):
                h_send[tile, pl.ds(k, GY, stride=8), :] = swapped[k]

        for t in range(2):
            pack(2 * h + t, [line(h, t * 8 + b) for b in range(8)])
        if h == CHUNKS - 1:
            pack(SHARED_BACK, [line(chunk, 16 + e) for chunk in range(CHUNKS) for e in range(2)])

    def gather(tile, places):
        swapped = block_swap([b_recv[tile, i * 16 : (i + 1) * 16, :] for i in range(GZ)])
        for (h, row), piece in zip(places, swapped, strict=True):
            high, low = halves(piece)
            back_left[h, row * 16 : (row + 1) * 16, 0:128] = high
            back_left[h, row * 16 : (row + 1) * 16, 128:256] = low

    def x_inverse(h):
        for t in range(2):
            gather(2 * h + t, [(h, group_row(c2, t * 8 + b)) for c2 in range(2) for b in range(8)])
        value = dot_left(back_left[h, 64:576, :], x_back.at[h], slice(0, NX))
        x_spec[64:576, :] = value if h == 0 else x_spec[64:576, :] + value

    def x_shared():
        gather(
            SHARED_BACK,
            [(h, group_row(c2, 16 + e)) for c2 in range(2) for h in range(CHUNKS) for e in range(2)],
        )
        x_spec[0:64, :] = sum(dot_left(back_left[h, 0:64, :], x_back.at[h], slice(0, NX)) for h in range(CHUNKS))

    for load in loads[1:]:
        load.wait()

    def stage_z(h):
        to_z[h][1]()
        z_transform(z_fwd, f_recv, g_send, FORWARD[h])
        to_y[h][0]()

    def stage_y(h):
        to_y[h][1]()
        y_transform(h)
        green(h)
        y_inverse(h)
        from_y[h][0]()

    def stage_back(h):
        from_y[h][1]()
        z_transform(z_back, h_recv, b_send, BACKWARD[h])
        from_z[h][0]()

    def stage_x(h):
        from_z[h][1]()
        x_inverse(h)

    stage_z(0)
    stage_z(1)
    stage_y(0)
    stage_z(2)
    stage_y(1)
    stage_back(0)
    stage_z(3)
    stage_y(2)
    stage_back(1)
    stage_y(3)
    stage_back(2)
    stage_x(0)
    stage_back(3)
    stage_x(1)
    stage_x(2)
    for group in (to_z, to_y, from_y, from_z):
        for h in range(CHUNKS - (group is from_z)):
            group[h][2]()
    stage_x(3)
    x_shared()
    for c in range(6):
        for y in range(YL):
            row = group_row(c % 2, c // 2 * YL + y) * 16
            out[c, y] = x_spec[row : row + ZL, :]
    from_z[CHUNKS - 1][2]()


def local(strain, phase, density, target):
    consts = [jnp.asarray(table) for table in tables()]
    vmem = pl.BlockSpec(memory_space=pltpu.VMEM)
    smem = pl.BlockSpec(memory_space=pltpu.SMEM)
    hbm = pl.BlockSpec(memory_space=pl.ANY)
    dma = pltpu.SemaphoreType.DMA
    return pl.pallas_call(
        kernel,
        out_shape=jax.ShapeDtypeStruct((6, YL, ZL, NX), F32),
        in_specs=[vmem, vmem, smem, smem] + [hbm] * 6,
        out_specs=vmem,
        scratch_shapes=[pltpu.VMEM(table.shape, BF16) for table in consts]
        + [
            pltpu.VMEM((36, 16, NX), F32),
            pltpu.VMEM((576, 2 * NX), BF16),
            pltpu.VMEM((576, NX), F32),
        ]
        + [pltpu.VMEM((TILES, 256, 128), F32)] * 8
        + [
            pltpu.VMEM((1024, 384), BF16),
            pltpu.VMEM((4 * NY, 384), BF16),
            pltpu.VMEM((NY, 384), F32),
            pltpu.VMEM((CHUNKS, NY, 384), F32),
            pltpu.VMEM((CHUNKS, 576, 256), BF16),
        ]
        + [dma((6,))]
        + [dma((CHUNKS,))] * 8,
        compiler_params=pltpu.CompilerParams(collective_id=0, has_side_effects=True, vmem_limit_bytes=56 * 2**20),
        cost_estimate=pl.CostEstimate(flops=3_500_000_000, bytes_accessed=8_000_000, transcendentals=0),
    )(strain, phase, density, target, *consts)


def solution(mesh):
    placed = (P(None, "gy", "gz", None), P("gy", "gz", None), P(), P())
    return jax.shard_map(local, mesh=mesh, in_specs=placed, out_specs=P(None, "gy", "gz", None), check_vma=False)
```

```python
import math

import jax
import jax.numpy as jnp
import ml_dtypes
import numpy as np
from jax import lax
from jax.experimental import pallas as pl
from jax.experimental.pallas import tpu as pltpu
from jax.sharding import PartitionSpec as P

NX, NY, NZ = 512, 192, 192
GY, GZ = 32, 16
YL, ZL = NY // GY, NZ // GZ
VOXELS = float(NX * NY * NZ)
LAME_SOLID = 0.5769230769
SHEAR_SOLID = 0.3846153846
MESH = pl.DeviceIdType.MESH
F32, BF16 = jnp.float32, jnp.bfloat16
TILES = 9
CHUNKS = 4
FORWARD = ((0, 3), (3, 5), (5, 7), (7, 9))
BACKWARD = ((0, 2), (2, 4), (4, 6), (6, 9))
SHARED_FORWARD, SHARED_BACK = 2, 8


def forward_tile(h, t):
    return t if h == 0 else 1 + 2 * h + t


def group_row(c2, m):
    return c2 * 2 + m - 16 if m >= 16 else 4 + c2 * 16 + m


def split_table(table, axis):
    high = table.astype(np.float32).astype(ml_dtypes.bfloat16)
    low = (table - high.astype(np.float64)).astype(np.float32).astype(ml_dtypes.bfloat16)
    return np.concatenate([high, high, low], axis=axis)


def wave(rows, columns, length):
    angle = 2.0 * math.pi / length * ((np.asarray(rows)[:, None] * np.asarray(columns)[None, :]) % length)
    return np.cos(angle), np.sin(angle)


def tables():
    kx = np.array([d * 16 + h * 4 + k for h in range(CHUNKS) for d in range(GZ) for _ in range(2) for k in range(4)])
    imag = np.array([r for _ in range(CHUNKS) for _ in range(GZ) for r in range(2) for _ in range(4)])
    cosine, sine = wave(np.arange(NX), kx, NX)
    x_table = np.where(imag[None, :] == 0, cosine, -sine)
    x_forward = split_table(x_table, 0)
    x_back = np.stack([split_table(x_table.T[h * 128 : (h + 1) * 128], 0) for h in range(CHUNKS)])

    z_rows = np.arange(GZ * 16)
    z_of, z_ok = (z_rows // 16) * ZL + np.minimum(z_rows % 16, ZL - 1), z_rows % 16 < ZL
    k_rows = np.arange(GY * 8)
    k_of, k_ok = (k_rows // 8) * 6 + np.minimum(k_rows % 8, 5), k_rows % 8 < 6
    cosine, sine = wave(k_of, z_of, NZ)
    ok = k_ok[:, None] & z_ok[None, :]
    cosine, sine = np.where(ok, cosine, 0.0), np.where(ok, sine, 0.0)
    z_forward = split_table(np.concatenate([cosine, sine], axis=1), 1)
    z_back = split_table(np.concatenate([cosine.T, -sine.T], axis=1), 1)

    y_of = np.array([s * YL + y for y in range(YL) for s in range(GY)])
    cosine, sine = wave(np.arange(NY), y_of, NY)
    y_forward = split_table(np.concatenate([cosine, sine], axis=1), 1)
    y_back = split_table(np.concatenate([cosine.T, -sine.T], axis=1), 1)
    return x_forward, z_forward, y_forward, y_back, z_back, x_back


def lane_ids(rows):
    return lax.broadcasted_iota(jnp.int32, (rows, 128), 1)


def block_swap(arrays, width=8):
    lane = lane_ids(arrays[0].shape[0])
    step = len(arrays) // 2
    while step:
        shift = width * step
        low = (lane // shift) % 2 == 0
        out = list(arrays)
        for i in range(len(arrays)):
            if (i // step) % 2 == 0:
                a, b = arrays[i], arrays[i + step]
                out[i] = jnp.where(low, a, pltpu.roll(b, shift, 1))
                out[i + step] = jnp.where(low, pltpu.roll(a, 128 - shift, 1), b)
        arrays, step = out, step // 2
    return arrays


def pair_swap(a, b):
    low = lane_ids(a.shape[0]) < 64
    return jnp.where(low, a, pltpu.roll(b, 64, 1)), jnp.where(low, pltpu.roll(a, 64, 1), b)


def turned(x):
    real = (lane_ids(x.shape[0]) // 4) % 2 == 0
    return jnp.where(real, pltpu.roll(x, 124, 1), -pltpu.roll(x, 4, 1))


def halves(x):
    high = x.astype(BF16)
    return high, (x - high.astype(F32)).astype(BF16)


def put_operand(ref, row, count, lanes, x):
    high, low = halves(x)
    turn_high, turn_low = halves(turned(x))
    size = x.shape[0]
    for block, value in enumerate((high, turn_high, low, turn_low)):
        ref[pl.ds(row + block * count, size), lanes] = value


def dot(a, b):
    return jnp.dot(a, b, preferred_element_type=F32)


def dot_right(table, ref, lanes):
    cut = ref.shape[0]
    return dot(table[:, 0:cut], ref[:, lanes]) + dot(table[:, cut:], ref[0 : cut // 2, lanes])


def dot_left(left, table, lanes):
    cut = left.shape[1]
    return dot(left, table[0:cut, lanes]) + dot(left[:, 0 : cut // 2], table[cut:, lanes])


def kernel(
    strain_hbm, phase_hbm, density, target, x_table_hbm, z_fwd_hbm, y_fwd_hbm, y_back_hbm, z_back_hbm, x_back_hbm,
    out,
    strain, phase, x_table, z_fwd, y_fwd, y_back, z_back, x_back,
    field, x_left, x_spec,
    f_send, f_recv, g_send, g_recv, h_send, h_recv, b_send, b_recv,
    z_right, y_right, y_spec, y_lines, back_left,
    table_sem, f_ssem, f_rsem, g_ssem, g_rsem, h_ssem, h_rsem, b_ssem, b_rsem,
):
    gy, gz = lax.axis_index("gy"), lax.axis_index("gz")

    loads = [
        pltpu.make_async_copy(src, dst, table_sem.at[i])
        for i, (src, dst) in enumerate(
            ((strain_hbm, strain), (phase_hbm, phase), (x_table_hbm, x_table), (z_fwd_hbm, z_fwd), (y_fwd_hbm, y_fwd), (y_back_hbm, y_back), (z_back_hbm, z_back), (x_back_hbm, x_back))
        )
    ]
    for load in loads:
        load.start()

    barrier = pltpu.get_barrier_semaphore()

    def greet(axis, me, n):
        def body(i, carry):
            pl.semaphore_signal(barrier, inc=1, device_id={axis: lax.rem(me + i, n)}, device_id_type=MESH)
            return carry

        lax.fori_loop(1, n, body, 0)

    greet("gz", gz, GZ)
    greet("gy", gy, GY)

    for i in range(GZ):
        f_recv[:, i * 16 + ZL : (i + 1) * 16, :] = jnp.zeros((TILES, 16 - ZL, 128), F32)
    for i in range(GY):
        h_recv[:, i * 8 + 6 : (i + 1) * 8, :] = jnp.zeros((TILES, 2, 128), F32)

    def transfer(axis, me, n, pad, used, src, dst, ssem, rsem, chunk, tiles):
        lo, hi = tiles

        def copy(i):
            hop = n // 2 - lax.div(i, 2)
            there = lax.rem(me + jnp.where(lax.rem(i, 2) == 1, hop, n - hop), n)
            return pltpu.make_async_remote_copy(
                src_ref=src.at[lo:hi, pl.ds(pl.multiple_of(there * pad, pad), used), :],
                dst_ref=dst.at[lo:hi, pl.ds(pl.multiple_of(me * pad, pad), used), :],
                send_sem=ssem.at[chunk],
                recv_sem=rsem.at[chunk],
                device_id={axis: there},
                device_id_type=MESH,
            )

        def start():
            lax.fori_loop(1, n, lambda i, c: (copy(i).start(), c)[1], 0)
            own = pl.ds(pl.multiple_of(me * pad, pad), used)
            dst[lo:hi, own, :] = src[lo:hi, own, :]

        def all_copies():
            rows = (n - 1) * used
            return pltpu.make_async_remote_copy(
                src_ref=src.at[lo:hi, 0:rows, :],
                dst_ref=dst.at[lo:hi, 0:rows, :],
                send_sem=ssem.at[chunk],
                recv_sem=rsem.at[chunk],
                device_id={axis: lax.rem(me + 1, n)},
                device_id_type=MESH,
            )

        def wait_recv():
            all_copies().wait_recv()

        def wait_send():
            all_copies().wait_send()

        return start, wait_recv, wait_send

    to_z = [transfer("gz", gz, GZ, 16, ZL, f_send, f_recv, f_ssem, f_rsem, h, FORWARD[h]) for h in range(CHUNKS)]
    to_y = [transfer("gy", gy, GY, 8, 6, g_send, g_recv, g_ssem, g_rsem, h, FORWARD[h]) for h in range(CHUNKS)]
    from_y = [transfer("gy", gy, GY, 8, 6, h_send, h_recv, h_ssem, h_rsem, h, BACKWARD[h]) for h in range(CHUNKS)]
    from_z = [transfer("gz", gz, GZ, 16, ZL, b_send, b_recv, b_ssem, b_rsem, h, BACKWARD[h]) for h in range(CHUNKS)]

    cubes = [density[i] * density[i] * density[i] for i in range(16)]
    least, most = cubes[0], cubes[0]
    for value in cubes[1:]:
        least, most = jnp.minimum(least, value), jnp.maximum(most, value)
    middle = 0.5 * (least + most)
    lame_ref, shear_ref = LAME_SOLID * middle, SHEAR_SOLID * middle

    field[...] = jnp.zeros_like(field)
    loads[0].wait()
    loads[1].wait()

    def polarize(y, carry):
        level = phase[y]
        stiff = jnp.zeros(level.shape, F32)
        for i, value in enumerate(cubes):
            stiff = jnp.where(level == i, value, stiff)
        excess = stiff - middle
        parts = [strain[c, y] for c in range(6)]
        trace = LAME_SOLID * (parts[0] + parts[1] + parts[2])
        for c in range(6):
            value = (2.0 * SHEAR_SOLID) * parts[c]
            m = (c // 2) * YL + y
            row = jnp.where(m >= 16, c % 2 * 2 + m - 16, 4 + c % 2 * 16 + m)
            field[row, 0:ZL, :] = excess * (value + trace if c < 3 else value)
        return carry

    lax.fori_loop(0, YL, polarize, 0)

    def split_rows(g, carry):
        high, low = halves(field[g])
        rows = pl.ds(pl.multiple_of(g * 16, 16), 16)
        x_left[rows, 0:512] = high
        x_left[rows, 512:1024] = low
        return carry

    lax.fori_loop(0, 36, split_rows, 0)

    def x_transform(rows, lanes):
        x_spec[rows, lanes] = dot_left(x_left[rows, :], x_table, lanes)

    def x_piece(c2, m, h):
        row = group_row(c2, m) * 16
        return x_spec[row : row + 16, h * 128 : (h + 1) * 128]

    def send_tile(tile, pieces):
        for i, piece in enumerate(block_swap(pieces)):
            f_send[tile, i * 16 : (i + 1) * 16, :] = piece

    def spread(h):
        for t in range(2):
            send_tile(forward_tile(h, t), [x_piece(c2, t * 8 + b, h) for c2 in range(2) for b in range(8)])

    loads[2].wait()
    x_transform(slice(0, 576), slice(0, 128))
    x_transform(slice(0, 64), slice(128, 512))
    spread(0)
    send_tile(SHARED_FORWARD, [x_piece(c2, 16 + e, h) for c2 in range(2) for h in range(CHUNKS) for e in range(2)])
    pl.semaphore_wait(barrier, GZ - 1 + GY - 1)
    to_z[0][0]()
    for h in range(1, CHUNKS):
        x_transform(slice(64, 576), slice(h * 128, (h + 1) * 128))
        spread(h)
        to_z[h][0]()

    def z_transform(table, source, result, tiles):
        lo, hi = tiles

        def fill(i, carry):
            lanes = pl.ds(pl.multiple_of(i * 128, 128), 128)
            for part in range(4):
                put_operand(z_right, part * 64, 256, lanes, source[lo + i, part * 64 : (part + 1) * 64, :])
            return carry

        lax.fori_loop(0, hi - lo, fill, 0)
        value = dot_right(table, z_right, slice(0, (hi - lo) * 128))
        for i in range(hi - lo):
            result[lo + i] = value[:, i * 128 : (i + 1) * 128]

    def y_transform(h):
        def unpack(tile):
            pieces = [g_recv[tile, pl.ds(k, GY, stride=8), :] for k in range(6)]
            return block_swap(pieces + [jnp.zeros((GY, 128), F32)] * 2)

        for t in range(3):
            swapped = unpack(forward_tile(h, t)) if t < 2 else unpack(SHARED_FORWARD)[h * 2 : h * 2 + 2]
            for b, piece in enumerate(swapped):
                cp, y = (t * 8 + b) // YL, (t * 8 + b) % YL
                put_operand(y_right, y * GY, NY, slice(cp * 128, (cp + 1) * 128), piece)
        y_spec[...] = dot_right(y_fwd, y_right, slice(0, 384))

    def green(h):
        rows = 16
        lane = lane_ids(1)
        k4, part, z8 = lane % 4, (lane // 4) % 2, (lane // 8) % 8
        wave_x = gz * 16 + h * 4 + k4
        wave_z = gy * 6 + z8
        signed_z = jnp.where(wave_z > NZ // 2, wave_z - NZ, wave_z)
        fx = jnp.broadcast_to(wave_x.astype(F32) / NX, (rows, 128))
        fz = jnp.broadcast_to(signed_z.astype(F32) / NZ, (rows, 128))
        lane_ok = (z8 < 6) & (wave_z != NZ // 2)
        weight = jnp.where(lane_ok, jnp.where(wave_x == 0, -1.0 / VOXELS, -2.0 / VOXELS), 0.0)
        origin = (wave_x == 0) & (wave_z == 0) & (z8 < 6)
        coupling = (lame_ref + shear_ref) / (shear_ref * (lame_ref + 2.0 * shear_ref))
        half_shear = 1.0 / (2.0 * shear_ref)

        def body(step, carry):
            start = pl.multiple_of(step * rows, rows)
            upper = pl.multiple_of(start + NY // 2, rows)
            wave_y = start + lax.broadcasted_iota(jnp.int32, (rows, 128), 0)
            wave_y = wave_y + jnp.where(lane_ids(rows) < 64, 0, NY // 2)
            fy = jnp.where(wave_y > NY // 2, wave_y - NY, wave_y).astype(F32) / NY
            zero = origin & (wave_y == 0)
            keep = (wave_y != NY // 2) & jnp.logical_not(zero)
            norm = jnp.where(zero, 1.0, fx * fx + fy * fy + fz * fz)
            inverse = 1.0 / norm
            scale = jnp.where(keep, weight * inverse, 0.0)
            s = []
            for cp in range(3):
                lanes = slice(cp * 128, (cp + 1) * 128)
                s += pair_swap(y_spec[pl.ds(start, rows), lanes], y_spec[pl.ds(upper, rows), lanes])
            vector = [
                fx * s[0] + fy * s[5] + fz * s[4],
                fx * s[5] + fy * s[1] + fz * s[3],
                fx * s[4] + fy * s[3] + fz * s[2],
            ]
            projected = fx * vector[0] + fy * vector[1] + fz * vector[2]
            fourth = (0.5 * coupling) * projected * inverse
            frequency = (fx, fy, fz)
            move = [scale * (half_shear * vector[i] - frequency[i] * fourth) for i in range(3)]
            images = [2.0 * frequency[i] * move[i] for i in range(3)]
            images += [frequency[i] * move[j] + frequency[j] * move[i] for i, j in ((1, 2), (0, 2), (0, 1))]
            real = (part == 0).astype(F32)
            gap = [target[c] * real - s[c] * (1.0 / VOXELS) for c in range(6)]
            gap_trace = (gap[0] + gap[1] + gap[2]) * (lame_ref / (3.0 * lame_ref + 2.0 * shear_ref))
            for c in range(6):
                macro = (gap[c] - gap_trace if c < 3 else gap[c]) * half_shear
                images[c] = jnp.where(zero, macro, images[c])
            for cp in range(3):
                lanes = slice(cp * 128, (cp + 1) * 128)
                first, second = pair_swap(images[2 * cp], images[2 * cp + 1])
                put_operand(y_right, start, NY, lanes, first)
                put_operand(y_right, upper, NY, lanes, second)
            return carry

        lax.fori_loop(0, NY // 2 // rows, body, 0)

    def y_inverse(h):
        y_lines[h] = dot_right(y_back, y_right, slice(0, 384))

        def line(chunk, m):
            cp, y = m // YL, m % YL
            return y_lines[chunk, y * GY : (y + 1) * GY, cp * 128 : (cp + 1) * 128]

        def pack(tile, pieces):
            swapped = block_swap(pieces)
            for k in range(6):
                h_send[tile, pl.ds(k, GY, stride=8), :] = swapped[k]

        for t in range(2):
            pack(2 * h + t, [line(h, t * 8 + b) for b in range(8)])
        if h == CHUNKS - 1:
            pack(SHARED_BACK, [line(chunk, 16 + e) for chunk in range(CHUNKS) for e in range(2)])

    def gather(tile, places):
        swapped = block_swap([b_recv[tile, i * 16 : (i + 1) * 16, :] for i in range(GZ)])
        for (h, row), piece in zip(places, swapped, strict=True):
            high, low = halves(piece)
            back_left[h, row * 16 : (row + 1) * 16, 0:128] = high
            back_left[h, row * 16 : (row + 1) * 16, 128:256] = low

    def x_inverse(h):
        for t in range(2):
            gather(2 * h + t, [(h, group_row(c2, t * 8 + b)) for c2 in range(2) for b in range(8)])
        value = dot_left(back_left[h, 64:576, :], x_back.at[h], slice(0, NX))
        x_spec[64:576, :] = value if h == 0 else x_spec[64:576, :] + value

    def x_shared():
        gather(
            SHARED_BACK,
            [(h, group_row(c2, 16 + e)) for c2 in range(2) for h in range(CHUNKS) for e in range(2)],
        )
        x_spec[0:64, :] = sum(dot_left(back_left[h, 0:64, :], x_back.at[h], slice(0, NX)) for h in range(CHUNKS))

    for load in loads[3:]:
        load.wait()

    def stage_z(h):
        to_z[h][1]()
        z_transform(z_fwd, f_recv, g_send, FORWARD[h])
        to_y[h][0]()

    def stage_y(h):
        to_y[h][1]()
        y_transform(h)
        green(h)
        y_inverse(h)
        from_y[h][0]()

    def stage_back(h):
        from_y[h][1]()
        z_transform(z_back, h_recv, b_send, BACKWARD[h])
        from_z[h][0]()

    def stage_x(h):
        from_z[h][1]()
        x_inverse(h)

    stage_z(0)
    stage_z(1)
    stage_y(0)
    stage_z(2)
    stage_y(1)
    stage_back(0)
    stage_z(3)
    stage_y(2)
    stage_back(1)
    stage_y(3)
    stage_back(2)
    stage_x(0)
    stage_back(3)
    stage_x(1)
    stage_x(2)
    for group in (to_z, to_y, from_y, from_z):
        for h in range(CHUNKS - (group is from_z)):
            group[h][2]()
    stage_x(3)
    x_shared()
    for c in range(6):
        for y in range(YL):
            row = group_row(c % 2, c // 2 * YL + y) * 16
            out[c, y] = x_spec[row : row + ZL, :]
    from_z[CHUNKS - 1][2]()


def local(strain, phase, density, target):
    consts = [jnp.asarray(table) for table in tables()]
    vmem = pl.BlockSpec(memory_space=pltpu.VMEM)
    smem = pl.BlockSpec(memory_space=pltpu.SMEM)
    hbm = pl.BlockSpec(memory_space=pltpu.HBM)
    dma = pltpu.SemaphoreType.DMA
    return pl.pallas_call(
        kernel,
        out_shape=pltpu.VMEM((6, YL, ZL, NX), F32),
        in_specs=[hbm, hbm, smem, smem] + [hbm] * 6,
        out_specs=vmem,
        scratch_shapes=[pltpu.VMEM((6, YL, ZL, NX), F32), pltpu.VMEM((YL, ZL, NX), jnp.int32)]
        + [pltpu.VMEM(table.shape, BF16) for table in consts]
        + [
            pltpu.VMEM((36, 16, NX), F32),
            pltpu.VMEM((576, 2 * NX), BF16),
            pltpu.VMEM((576, NX), F32),
        ]
        + [pltpu.VMEM((TILES, 256, 128), F32)] * 8
        + [
            pltpu.VMEM((1024, 384), BF16),
            pltpu.VMEM((4 * NY, 384), BF16),
            pltpu.VMEM((NY, 384), F32),
            pltpu.VMEM((CHUNKS, NY, 384), F32),
            pltpu.VMEM((CHUNKS, 576, 256), BF16),
        ]
        + [dma((8,))]
        + [dma((CHUNKS,))] * 8,
        compiler_params=pltpu.CompilerParams(collective_id=0, has_side_effects=True, vmem_limit_bytes=56 * 2**20),
        cost_estimate=pl.CostEstimate(flops=3_500_000_000, bytes_accessed=8_000_000, transcendentals=0),
    )(strain, phase, density, target, *consts)


def solution(mesh):
    placed = (P(None, "gy", "gz", None), P("gy", "gz", None), P(), P())
    return jax.shard_map(local, mesh=mesh, in_specs=placed, out_specs=P(None, "gy", "gz", None), check_vma=False)
```

```python
import math

import jax
import jax.numpy as jnp
import ml_dtypes
import numpy as np
from jax import lax
from jax.experimental import pallas as pl
from jax.experimental.pallas import tpu as pltpu
from jax.sharding import PartitionSpec as P

NX, NY, NZ = 512, 192, 192
GY, GZ = 32, 16
YL, ZL = NY // GY, NZ // GZ
VOXELS = float(NX * NY * NZ)
LAME_SOLID = 0.5769230769
SHEAR_SOLID = 0.3846153846
MESH = pl.DeviceIdType.MESH
F32, BF16 = jnp.float32, jnp.bfloat16
TILES = 9
CHUNKS = 4
FORWARD = ((0, 3), (3, 5), (5, 7), (7, 9))
BACKWARD = ((0, 2), (2, 4), (4, 6), (6, 9))
SHARED_FORWARD, SHARED_BACK = 2, 8


def forward_tile(h, t):
    return t if h == 0 else 1 + 2 * h + t


def group_row(c2, m):
    return c2 * 2 + m - 16 if m >= 16 else 4 + c2 * 16 + m


def split_table(table, axis):
    high = table.astype(np.float32).astype(ml_dtypes.bfloat16)
    low = (table - high.astype(np.float64)).astype(np.float32).astype(ml_dtypes.bfloat16)
    return np.concatenate([high, high, low], axis=axis)


def wave(rows, columns, length):
    angle = 2.0 * math.pi / length * ((np.asarray(rows)[:, None] * np.asarray(columns)[None, :]) % length)
    return np.cos(angle), np.sin(angle)


def tables():
    kx = np.array([d * 16 + h * 4 + k for h in range(CHUNKS) for d in range(GZ) for _ in range(2) for k in range(4)])
    imag = np.array([r for _ in range(CHUNKS) for _ in range(GZ) for r in range(2) for _ in range(4)])
    cosine, sine = wave(np.arange(NX), kx, NX)
    x_table = np.where(imag[None, :] == 0, cosine, -sine)
    x_forward = split_table(x_table, 0)
    x_back = np.stack([split_table(x_table.T[h * 128 : (h + 1) * 128], 0) for h in range(CHUNKS)])

    z_rows = np.arange(GZ * 16)
    z_of, z_ok = (z_rows // 16) * ZL + np.minimum(z_rows % 16, ZL - 1), z_rows % 16 < ZL
    k_rows = np.arange(GY * 8)
    k_of, k_ok = (k_rows // 8) * 6 + np.minimum(k_rows % 8, 5), k_rows % 8 < 6
    cosine, sine = wave(k_of, z_of, NZ)
    ok = k_ok[:, None] & z_ok[None, :]
    cosine, sine = np.where(ok, cosine, 0.0), np.where(ok, sine, 0.0)
    z_forward = split_table(np.concatenate([cosine, sine], axis=1), 1)
    z_back = split_table(np.concatenate([cosine.T, -sine.T], axis=1), 1)

    y_of = np.array([s * YL + y for y in range(YL) for s in range(GY)])
    cosine, sine = wave(np.arange(NY), y_of, NY)
    y_forward = split_table(np.concatenate([cosine, sine], axis=1), 1)
    y_back = split_table(np.concatenate([cosine.T, -sine.T], axis=1), 1)
    return x_forward, z_forward, y_forward, y_back, z_back, x_back


def lane_ids(rows):
    return lax.broadcasted_iota(jnp.int32, (rows, 128), 1)


def block_swap(arrays, width=8):
    lane = lane_ids(arrays[0].shape[0])
    step = len(arrays) // 2
    while step:
        shift = width * step
        low = (lane // shift) % 2 == 0
        out = list(arrays)
        for i in range(len(arrays)):
            if (i // step) % 2 == 0:
                a, b = arrays[i], arrays[i + step]
                out[i] = jnp.where(low, a, pltpu.roll(b, shift, 1))
                out[i + step] = jnp.where(low, pltpu.roll(a, 128 - shift, 1), b)
        arrays, step = out, step // 2
    return arrays


def pair_swap(a, b):
    low = lane_ids(a.shape[0]) < 64
    return jnp.where(low, a, pltpu.roll(b, 64, 1)), jnp.where(low, pltpu.roll(a, 64, 1), b)


def turned(x):
    real = (lane_ids(x.shape[0]) // 4) % 2 == 0
    return jnp.where(real, pltpu.roll(x, 124, 1), -pltpu.roll(x, 4, 1))


def halves(x):
    high = x.astype(BF16)
    return high, (x - high.astype(F32)).astype(BF16)


def put_operand(ref, row, count, lanes, x):
    high, low = halves(x)
    turn_high, turn_low = halves(turned(x))
    size = x.shape[0]
    for block, value in enumerate((high, turn_high, low, turn_low)):
        ref[pl.ds(row + block * count, size), lanes] = value


def dot(a, b):
    return jnp.dot(a, b, preferred_element_type=F32)


def dot_right(table, ref, lanes):
    cut = ref.shape[0]
    return dot(table[:, 0:cut], ref[:, lanes]) + dot(table[:, cut:], ref[0 : cut // 2, lanes])


def dot_left(left, table, lanes):
    cut = left.shape[1]
    return dot(left, table[0:cut, lanes]) + dot(left[:, 0 : cut // 2], table[cut:, lanes])


def kernel(
    strain_hbm, phase_hbm, density, target, x_table_hbm, z_fwd_hbm, y_fwd_hbm, y_back_hbm, z_back_hbm, x_back_hbm,
    out,
    strain, phase, x_table, z_fwd, y_fwd, y_back, z_back, x_back,
    field, x_left, x_spec,
    f_send, f_recv, g_send, g_recv, h_send, h_recv, b_send, b_recv,
    z_right, y_right, y_spec, y_lines, back_left,
    table_sem, f_ssem, f_rsem, g_ssem, g_rsem, h_ssem, h_rsem, b_ssem, b_rsem,
):
    gy, gz = lax.axis_index("gy"), lax.axis_index("gz")

    loads = [
        pltpu.make_async_copy(src, dst, table_sem.at[i])
        for i, (src, dst) in enumerate(
            ((strain_hbm, strain), (phase_hbm, phase), (x_table_hbm, x_table), (z_fwd_hbm, z_fwd), (y_fwd_hbm, y_fwd), (y_back_hbm, y_back), (z_back_hbm, z_back), (x_back_hbm, x_back))
        )
    ]
    for load in loads:
        load.start()

    barrier = pltpu.get_barrier_semaphore()

    def greet(axis, me, n):
        def body(i, carry):
            pl.semaphore_signal(barrier, inc=1, device_id={axis: lax.rem(me + i, n)}, device_id_type=MESH)
            return carry

        lax.fori_loop(1, n, body, 0)

    greet("gz", gz, GZ)
    greet("gy", gy, GY)

    for i in range(GZ):
        f_recv[:, i * 16 + ZL : (i + 1) * 16, :] = jnp.zeros((TILES, 16 - ZL, 128), F32)
    for i in range(GY):
        h_recv[:, i * 8 + 6 : (i + 1) * 8, :] = jnp.zeros((TILES, 2, 128), F32)

    def transfer(axis, me, n, pad, used, src, dst, ssem, rsem, chunk, tiles):
        lo, hi = tiles

        def far_first(i):
            hop = n // 2 - lax.div(i, 2)
            return lax.rem(me + jnp.where(lax.rem(i, 2) == 1, hop, n - hop), n)

        def start_ordered(i, carry):
            quarter = lax.div(i, 4)
            quarter = lax.rem(quarter, 2) * 2 + lax.div(quarter, 2)
            there = quarter * 4 + lax.rem(me + i, 4)

            @pl.when(there != me)
            def _():
                copy_to(there).start()

            return carry

        def copy_to(there):
            return pltpu.make_async_remote_copy(
                src_ref=src.at[lo:hi, pl.ds(pl.multiple_of(there * pad, pad), used), :],
                dst_ref=dst.at[lo:hi, pl.ds(pl.multiple_of(me * pad, pad), used), :],
                send_sem=ssem.at[chunk],
                recv_sem=rsem.at[chunk],
                device_id={axis: there},
                device_id_type=MESH,
            )

        def start():
            if src is b_send and chunk == CHUNKS - 1:
                lax.fori_loop(0, n, start_ordered, 0)
            else:
                lax.fori_loop(1, n, lambda i, c: (copy_to(far_first(i)).start(), c)[1], 0)
            own = pl.ds(pl.multiple_of(me * pad, pad), used)
            dst[lo:hi, own, :] = src[lo:hi, own, :]

        def all_copies():
            rows = (n - 1) * used
            return pltpu.make_async_remote_copy(
                src_ref=src.at[lo:hi, 0:rows, :],
                dst_ref=dst.at[lo:hi, 0:rows, :],
                send_sem=ssem.at[chunk],
                recv_sem=rsem.at[chunk],
                device_id={axis: lax.rem(me + 1, n)},
                device_id_type=MESH,
            )

        def wait_recv():
            all_copies().wait_recv()

        def wait_send():
            all_copies().wait_send()

        return start, wait_recv, wait_send

    to_z = [transfer("gz", gz, GZ, 16, ZL, f_send, f_recv, f_ssem, f_rsem, h, FORWARD[h]) for h in range(CHUNKS)]
    to_y = [transfer("gy", gy, GY, 8, 6, g_send, g_recv, g_ssem, g_rsem, h, FORWARD[h]) for h in range(CHUNKS)]
    from_y = [transfer("gy", gy, GY, 8, 6, h_send, h_recv, h_ssem, h_rsem, h, BACKWARD[h]) for h in range(CHUNKS)]
    from_z = [transfer("gz", gz, GZ, 16, ZL, b_send, b_recv, b_ssem, b_rsem, h, BACKWARD[h]) for h in range(CHUNKS)]

    cubes = [density[i] * density[i] * density[i] for i in range(16)]
    least, most = cubes[0], cubes[0]
    for value in cubes[1:]:
        least, most = jnp.minimum(least, value), jnp.maximum(most, value)
    middle = 0.5 * (least + most)
    lame_ref, shear_ref = LAME_SOLID * middle, SHEAR_SOLID * middle

    field[...] = jnp.zeros_like(field)
    loads[0].wait()
    loads[1].wait()

    def polarize(y, carry):
        level = phase[y]
        stiff = jnp.zeros(level.shape, F32)
        for i, value in enumerate(cubes):
            stiff = jnp.where(level == i, value, stiff)
        excess = stiff - middle
        parts = [strain[c, y] for c in range(6)]
        trace = LAME_SOLID * (parts[0] + parts[1] + parts[2])
        for c in range(6):
            value = (2.0 * SHEAR_SOLID) * parts[c]
            m = (c // 2) * YL + y
            row = jnp.where(m >= 16, c % 2 * 2 + m - 16, 4 + c % 2 * 16 + m)
            field[row, 0:ZL, :] = excess * (value + trace if c < 3 else value)
        return carry

    lax.fori_loop(0, YL, polarize, 0)

    def split_rows(g, carry):
        high, low = halves(field[g])
        rows = pl.ds(pl.multiple_of(g * 16, 16), 16)
        x_left[rows, 0:512] = high
        x_left[rows, 512:1024] = low
        return carry

    lax.fori_loop(0, 36, split_rows, 0)

    def x_transform(rows, lanes):
        x_spec[rows, lanes] = dot_left(x_left[rows, :], x_table, lanes)

    def x_piece(c2, m, h):
        row = group_row(c2, m) * 16
        return x_spec[row : row + 16, h * 128 : (h + 1) * 128]

    def send_tile(tile, pieces):
        for i, piece in enumerate(block_swap(pieces)):
            f_send[tile, i * 16 : (i + 1) * 16, :] = piece

    def spread(h):
        for t in range(2):
            send_tile(forward_tile(h, t), [x_piece(c2, t * 8 + b, h) for c2 in range(2) for b in range(8)])

    loads[2].wait()
    x_transform(slice(0, 576), slice(0, 128))
    x_transform(slice(0, 64), slice(128, 512))
    spread(0)
    send_tile(SHARED_FORWARD, [x_piece(c2, 16 + e, h) for c2 in range(2) for h in range(CHUNKS) for e in range(2)])
    pl.semaphore_wait(barrier, GZ - 1 + GY - 1)
    to_z[0][0]()
    for h in range(1, CHUNKS):
        x_transform(slice(64, 576), slice(h * 128, (h + 1) * 128))
        spread(h)
        to_z[h][0]()

    def z_transform(table, source, result, tiles):
        lo, hi = tiles

        def fill(i, carry):
            lanes = pl.ds(pl.multiple_of(i * 128, 128), 128)
            for part in range(4):
                put_operand(z_right, part * 64, 256, lanes, source[lo + i, part * 64 : (part + 1) * 64, :])
            return carry

        lax.fori_loop(0, hi - lo, fill, 0)
        value = dot_right(table, z_right, slice(0, (hi - lo) * 128))
        for i in range(hi - lo):
            result[lo + i] = value[:, i * 128 : (i + 1) * 128]

    def y_transform(h):
        def unpack(tile):
            pieces = [g_recv[tile, pl.ds(k, GY, stride=8), :] for k in range(6)]
            return block_swap(pieces + [jnp.zeros((GY, 128), F32)] * 2)

        for t in range(3):
            swapped = unpack(forward_tile(h, t)) if t < 2 else unpack(SHARED_FORWARD)[h * 2 : h * 2 + 2]
            for b, piece in enumerate(swapped):
                cp, y = (t * 8 + b) // YL, (t * 8 + b) % YL
                put_operand(y_right, y * GY, NY, slice(cp * 128, (cp + 1) * 128), piece)
        y_spec[...] = dot_right(y_fwd, y_right, slice(0, 384))

    def green(h):
        rows = 16
        lane = lane_ids(1)
        k4, part, z8 = lane % 4, (lane // 4) % 2, (lane // 8) % 8
        wave_x = gz * 16 + h * 4 + k4
        wave_z = gy * 6 + z8
        signed_z = jnp.where(wave_z > NZ // 2, wave_z - NZ, wave_z)
        fx = jnp.broadcast_to(wave_x.astype(F32) / NX, (rows, 128))
        fz = jnp.broadcast_to(signed_z.astype(F32) / NZ, (rows, 128))
        lane_ok = (z8 < 6) & (wave_z != NZ // 2)
        weight = jnp.where(lane_ok, jnp.where(wave_x == 0, -1.0 / VOXELS, -2.0 / VOXELS), 0.0)
        origin = (wave_x == 0) & (wave_z == 0) & (z8 < 6)
        coupling = (lame_ref + shear_ref) / (shear_ref * (lame_ref + 2.0 * shear_ref))
        half_shear = 1.0 / (2.0 * shear_ref)

        def body(step, carry):
            start = pl.multiple_of(step * rows, rows)
            upper = pl.multiple_of(start + NY // 2, rows)
            wave_y = start + lax.broadcasted_iota(jnp.int32, (rows, 128), 0)
            wave_y = wave_y + jnp.where(lane_ids(rows) < 64, 0, NY // 2)
            fy = jnp.where(wave_y > NY // 2, wave_y - NY, wave_y).astype(F32) / NY
            zero = origin & (wave_y == 0)
            keep = (wave_y != NY // 2) & jnp.logical_not(zero)
            norm = jnp.where(zero, 1.0, fx * fx + fy * fy + fz * fz)
            inverse = 1.0 / norm
            scale = jnp.where(keep, weight * inverse, 0.0)
            s = []
            for cp in range(3):
                lanes = slice(cp * 128, (cp + 1) * 128)
                s += pair_swap(y_spec[pl.ds(start, rows), lanes], y_spec[pl.ds(upper, rows), lanes])
            vector = [
                fx * s[0] + fy * s[5] + fz * s[4],
                fx * s[5] + fy * s[1] + fz * s[3],
                fx * s[4] + fy * s[3] + fz * s[2],
            ]
            projected = fx * vector[0] + fy * vector[1] + fz * vector[2]
            fourth = (0.5 * coupling) * projected * inverse
            frequency = (fx, fy, fz)
            move = [scale * (half_shear * vector[i] - frequency[i] * fourth) for i in range(3)]
            images = [2.0 * frequency[i] * move[i] for i in range(3)]
            images += [frequency[i] * move[j] + frequency[j] * move[i] for i, j in ((1, 2), (0, 2), (0, 1))]
            real = (part == 0).astype(F32)
            gap = [target[c] * real - s[c] * (1.0 / VOXELS) for c in range(6)]
            gap_trace = (gap[0] + gap[1] + gap[2]) * (lame_ref / (3.0 * lame_ref + 2.0 * shear_ref))
            for c in range(6):
                macro = (gap[c] - gap_trace if c < 3 else gap[c]) * half_shear
                images[c] = jnp.where(zero, macro, images[c])
            for cp in range(3):
                lanes = slice(cp * 128, (cp + 1) * 128)
                first, second = pair_swap(images[2 * cp], images[2 * cp + 1])
                put_operand(y_right, start, NY, lanes, first)
                put_operand(y_right, upper, NY, lanes, second)
            return carry

        lax.fori_loop(0, NY // 2 // rows, body, 0)

    def y_inverse(h):
        y_lines[h] = dot_right(y_back, y_right, slice(0, 384))

        def line(chunk, m):
            cp, y = m // YL, m % YL
            return y_lines[chunk, y * GY : (y + 1) * GY, cp * 128 : (cp + 1) * 128]

        def pack(tile, pieces):
            swapped = block_swap(pieces)
            for k in range(6):
                h_send[tile, pl.ds(k, GY, stride=8), :] = swapped[k]

        for t in range(2):
            pack(2 * h + t, [line(h, t * 8 + b) for b in range(8)])
        if h == CHUNKS - 1:
            pack(SHARED_BACK, [line(chunk, 16 + e) for chunk in range(CHUNKS) for e in range(2)])

    def gather(tile, places):
        swapped = block_swap([b_recv[tile, i * 16 : (i + 1) * 16, :] for i in range(GZ)])
        for (h, row), piece in zip(places, swapped, strict=True):
            high, low = halves(piece)
            back_left[h, row * 16 : (row + 1) * 16, 0:128] = high
            back_left[h, row * 16 : (row + 1) * 16, 128:256] = low

    def x_inverse(h):
        for t in range(2):
            gather(2 * h + t, [(h, group_row(c2, t * 8 + b)) for c2 in range(2) for b in range(8)])
        value = dot_left(back_left[h, 64:576, :], x_back.at[h], slice(0, NX))
        x_spec[64:576, :] = value if h == 0 else x_spec[64:576, :] + value

    def x_shared():
        gather(
            SHARED_BACK,
            [(h, group_row(c2, 16 + e)) for c2 in range(2) for h in range(CHUNKS) for e in range(2)],
        )
        x_spec[0:64, :] = sum(dot_left(back_left[h, 0:64, :], x_back.at[h], slice(0, NX)) for h in range(CHUNKS))

    for load in loads[3:]:
        load.wait()

    def stage_z(h):
        to_z[h][1]()
        z_transform(z_fwd, f_recv, g_send, FORWARD[h])
        to_y[h][0]()

    def stage_y(h):
        to_y[h][1]()
        y_transform(h)
        green(h)
        y_inverse(h)
        from_y[h][0]()

    def stage_back(h):
        from_y[h][1]()
        z_transform(z_back, h_recv, b_send, BACKWARD[h])
        from_z[h][0]()

    def stage_x(h):
        from_z[h][1]()
        x_inverse(h)

    stage_z(0)
    stage_z(1)
    stage_y(0)
    stage_z(2)
    stage_y(1)
    stage_back(0)
    stage_z(3)
    stage_y(2)
    stage_back(1)
    stage_y(3)
    stage_back(2)
    stage_x(0)
    stage_back(3)
    stage_x(1)
    stage_x(2)
    for group in (to_z, to_y, from_y, from_z):
        for h in range(CHUNKS - (group is from_z)):
            group[h][2]()
    stage_x(3)
    x_shared()
    for c in range(6):
        for y in range(YL):
            row = group_row(c % 2, c // 2 * YL + y) * 16
            out[c, y] = x_spec[row : row + ZL, :]
    from_z[CHUNKS - 1][2]()


def local(strain, phase, density, target):
    consts = [jnp.asarray(table) for table in tables()]
    vmem = pl.BlockSpec(memory_space=pltpu.VMEM)
    smem = pl.BlockSpec(memory_space=pltpu.SMEM)
    hbm = pl.BlockSpec(memory_space=pltpu.HBM)
    dma = pltpu.SemaphoreType.DMA
    return pl.pallas_call(
        kernel,
        out_shape=pltpu.VMEM((6, YL, ZL, NX), F32),
        in_specs=[hbm, hbm, smem, smem] + [hbm] * 6,
        out_specs=vmem,
        scratch_shapes=[pltpu.VMEM((6, YL, ZL, NX), F32), pltpu.VMEM((YL, ZL, NX), jnp.int32)]
        + [pltpu.VMEM(table.shape, BF16) for table in consts]
        + [
            pltpu.VMEM((36, 16, NX), F32),
            pltpu.VMEM((576, 2 * NX), BF16),
            pltpu.VMEM((576, NX), F32),
        ]
        + [pltpu.VMEM((TILES, 256, 128), F32)] * 8
        + [
            pltpu.VMEM((1024, 384), BF16),
            pltpu.VMEM((4 * NY, 384), BF16),
            pltpu.VMEM((NY, 384), F32),
            pltpu.VMEM((CHUNKS, NY, 384), F32),
            pltpu.VMEM((CHUNKS, 576, 256), BF16),
        ]
        + [dma((8,))]
        + [dma((CHUNKS,))] * 8,
        compiler_params=pltpu.CompilerParams(collective_id=0, has_side_effects=True, vmem_limit_bytes=56 * 2**20),
        cost_estimate=pl.CostEstimate(flops=3_500_000_000, bytes_accessed=8_000_000, transcendentals=0),
    )(strain, phase, density, target, *consts)


def solution(mesh):
    placed = (P(None, "gy", "gz", None), P("gy", "gz", None), P(), P())
    return jax.shard_map(local, mesh=mesh, in_specs=placed, out_specs=P(None, "gy", "gz", None), check_vma=False)
```
